128 devices in a mesh: dec: 32 (over z, x, core), seq: 4 (over y).
Axes of the slice: x: 4, y: 4, z: 4, core: 2. Of those that a mesh axis runs over, the one named last changes fastest.
Arguments:
- hidden_states: bfloat16 [1024, 7168], P(('dec', 'seq')), may hold values from -6 to 6
- gate_scores: float32 [1024, 8], P(('dec', 'seq')), may hold values from -6 to 6
- expert_ids: int32 [1024, 8], P(('dec', 'seq')), may hold values from 0 to 31, all different within a row; in each aligned block of 8 rows (0 to 7, 8 to 15, ...) at most 4 rows name the same one
- w_gate: bfloat16 [32, 7168, 2048], P('dec', None, 'seq'), may hold values from -0.0625 to 0.0625
- w_up: bfloat16 [32, 7168, 2048], P('dec', None, 'seq'), may hold values from -0.0625 to 0.0625
- w_down: bfloat16 [32, 2048, 7168], P('dec', 'seq'), may hold values from -0.125 to 0.125
- prefill_cache: bfloat16 [32, 1024, 576], P('dec', 'seq'), may hold values from -6 to 6
- plan: int32 [32], replicated, may hold values from 0 to 31, each once
- prompt_len: int32 [32], replicated, may hold values from 1 to 1024, 16384 in all
Outputs:
- moe_out: bfloat16 [1024, 7168], P(('dec', 'seq'))
- handed_cache: bfloat16 [32, 1024, 576], P('dec', 'seq')
The draws below stay inside these ranges and needn't reach their ends.
Inputs may be any that keep to these rules, and one draw needn't show every extreme that they name: `expert_ids`: each row names 8 different experts; among the rows of one device no expert is named more than 4 times. `plan`: each decode index is chosen by exactly one prefill group. `prompt_len`: some request has exactly 1024 prompt tokens.
All inputs are finite; a program needn't handle non-finite values.
Results may differ from the reference program's by a relative error of at most 0.0066.
Values may be sent and summed in bfloat16 or wider, within the bound.
A program may use at most 128 MiB of HBM per device.

```python
import math
import jax
import jax.numpy as jnp
import numpy as np
from jax import lax

D = 7168
FF = 2048
TOP = 8
LAT = 576
TOK_DEV = 8
EXPERTS = 32
CAP = 4
TOKENS = 1024
PMAX = 1024
N_DEC = 32
N_SEQ = 4


def shard_levels(rng, extent, pieces, low, high):
    def one(axis_at, shards_of):
        heights = jax.random.uniform(jax.random.fold_in(jax.random.fold_in(rng, 6), axis_at), (shards_of,), jnp.float32, low / len(pieces), high / len(pieces))
        return jnp.repeat(jnp.exp(heights), extent[axis_at] // shards_of).reshape((-1,) + (1,) * (len(extent) - axis_at - 1))

    gain = one(*pieces[0])
    for cut in pieces[1:]:
        gain = gain * one(*cut)
    return gain


def length_profile(amount, total, most, skew):
    loads = [(1 << 20) // math.isqrt(rank ** skew) + 1 for rank in range(2, amount + 1)]
    rest, counts = total - most - (amount - 1), [1] * (amount - 1)
    while rest > 0:
        free = [i for i in range(amount - 1) if counts[i] < most]
        mass, remaining = sum([loads[i] for i in free]), rest
        for i in free:
            extra = min(most - counts[i], max(1, remaining * loads[i] // mass), rest)
            counts[i] = counts[i] + extra
            rest = rest - extra
    return np.array([most] + counts)


def uneven(rng, number_of, total, reach, lean):
    if number_of == 2:
        one = jax.random.randint(rng, (), max(1, total - reach), min(reach, total - 1) + 1)
        return jnp.stack([one, total - one])
    sizes = jnp.asarray(length_profile(number_of, total, reach, lean), jnp.int32)
    twos = (number_of - 1) // 2
    source_of, taker = sizes[1:1 + 2 * twos:2], sizes[2:2 + 2 * twos:2]
    slack = jnp.minimum(source_of - 1, reach - taker)
    passed = jax.random.randint(jax.random.fold_in(rng, 1), (twos,), 0, 1 << 20) % (slack + 1)
    sizes = sizes.at[1:1 + 2 * twos:2].set(source_of - passed).at[2:2 + 2 * twos:2].set(taker + passed)
    return sizes[jax.random.permutation(jax.random.fold_in(rng, 2), number_of)]


def assign_block(stream_key, own, number, rows, number_of, top, most, slope):
    sequence = jax.random.permutation(stream_key, number_of)
    packed, common = portions_of(number_of, rows * top, most, slope, True), portions_of(number_of, rows * top, most, slope, False)
    places = jnp.arange(number_of)

    def named(sizes, rotation):
        used = int((sizes > 0).sum())
        fixed = max(1, used // 4)
        shifted = fixed + (places - fixed + rotation * (used - fixed)) % max(1, number_of - fixed)
        return jnp.zeros((number_of,), jnp.int32).at[sequence[jnp.where(places < fixed, places, shifted)]].set(jnp.asarray(sizes, jnp.int32))

    sizes = jnp.where(number % 4 == 0, named(packed, number // 4), named(common, number - number // 4 - 1))
    mixed = jax.random.permutation(jax.random.fold_in(own, 3), number_of)
    source_of, sink = mixed[0:number_of // 2 * 2:2], mixed[1:number_of // 2 * 2:2]
    margin = jnp.minimum(sizes[source_of] - 1, most - sizes[sink]) // 2
    margin = jnp.where((source_of == sequence[0]) | (sink == sequence[0]) | (sizes[sink] == 0), 0, jnp.maximum(margin, 0))
    shifted = jax.random.randint(jax.random.fold_in(own, 4), (number_of // 2,), 0, 1 << 20) % (margin + 1)
    sizes = sizes.at[source_of].add(-shifted).at[sink].add(shifted)
    items = jnp.searchsorted(jnp.cumsum(sizes), jnp.arange(rows * top), side="right").astype(jnp.int32)
    grid = items.reshape(top, rows).T
    grid = grid[jax.random.permutation(jax.random.fold_in(own, 1), rows)]
    rotation = jax.random.randint(jax.random.fold_in(own, 2), (rows, 1), 0, top)
    return jnp.take_along_axis(grid, (jnp.arange(top)[None, :] + rotation) % top, axis=1)


def portions_of(amount, total, bound, skew, full):
    portions = [(1 << 20) // math.isqrt(standing ** skew) + 1 for standing in range(1, amount + 1)]
    largest = bound if full else min(bound, max(-(-total // amount), total * portions[0] // sum(portions)))
    least = 1 if total - largest >= amount - 1 else 0
    holding, rest = [largest] + [least] * (amount - 1), total - largest - least * (amount - 1)
    while rest > 0:
        candidates = [i for i in range(1, amount) if holding[i] < largest] or [i for i in range(1, amount) if holding[i] < bound]
        whole, remaining = sum([portions[i] for i in candidates]), rest
        for i in candidates:
            addition = min(bound - holding[i], max(1, remaining * portions[i] // whole), rest)
            holding[i] = holding[i] + addition
            rest = rest - addition
    return np.array(holding)


def centred(stream_key, dims, deviation, bound, split=(), kind=jnp.bfloat16):
    gain = shard_levels(stream_key, dims, split, -0.22, 0.18) if split else 1.0
    array = jax.random.normal(stream_key, dims, jnp.float32) * deviation * gain
    return jnp.minimum(jnp.maximum(array, -bound), bound).astype(kind)


def setup_inputs(seed: int = 0) -> dict:
    keys = jax.random.split(jax.random.key(seed), 10)
    hidden_states = centred(keys[0], (TOKENS, D), 1.0, 6.0, ((0, 128),))
    gate_scores = centred(keys[1], (TOKENS, TOP), 1.5, 6.0, ((0, 128),), jnp.float32)
    expert_ids_keys = jax.random.split(jax.random.fold_in(keys[2], 1), TOKENS // TOK_DEV)
    expert_ids_turns = jax.random.permutation(jax.random.fold_in(keys[2], 3), TOKENS // TOK_DEV)
    expert_ids = jax.vmap(lambda own, number: assign_block(jax.random.fold_in(keys[2], 2), own, number, TOK_DEV, EXPERTS, TOP, CAP, 2))(expert_ids_keys, expert_ids_turns).reshape((TOKENS, TOP))
    w_gate = centred(keys[3], (EXPERTS, D, FF), D ** -0.5, 0.0625, ((0, 32), (2, 4)))
    w_up = centred(keys[4], (EXPERTS, D, FF), D ** -0.5, 0.0625, ((0, 32), (2, 4)))
    w_down = centred(keys[5], (EXPERTS, FF, D), FF ** -0.5, 0.125, ((0, 32), (1, 4)))
    prefill_cache = centred(keys[6], (N_DEC, PMAX, LAT), 1.0, 6.0, ((0, 32), (1, 4)))
    plan = jax.random.permutation(keys[7], N_DEC).astype(jnp.int32)
    prompt_len = uneven(keys[8], N_DEC, N_DEC * PMAX // 2, PMAX, 2).astype(jnp.int32)
    return dict(hidden_states=hidden_states, gate_scores=gate_scores, expert_ids=expert_ids, w_gate=w_gate, w_up=w_up, w_down=w_down, prefill_cache=prefill_cache, plan=plan, prompt_len=prompt_len)


def reference(hidden_states, gate_scores, expert_ids, w_gate, w_up, w_down, prefill_cache, plan, prompt_len):
    affinity = jax.nn.sigmoid(gate_scores.astype(jnp.float32))
    weight = 2.5 * affinity / jnp.sum(affinity, axis=1, keepdims=True)
    flat_ids = expert_ids.reshape(-1)
    flat_weight = weight.reshape(-1)
    assigned = TOKENS * TOP
    expert_rows = N_DEC * N_SEQ * CAP
    quarter = FF // N_SEQ

    def one_expert(combined, expert):
        assign_idx = jnp.nonzero(flat_ids == expert, size=expert_rows, fill_value=assigned)[0].astype(jnp.int32)
        is_live = assign_idx < assigned
        safe_idx = jnp.minimum(assign_idx, assigned - 1)
        token_idx = safe_idx // TOP
        routed_rows = hidden_states[token_idx]
        gate_proj = jnp.dot(routed_rows, w_gate[expert], preferred_element_type=jnp.float32)
        up_proj = jnp.dot(routed_rows, w_up[expert], preferred_element_type=jnp.float32)
        hidden = (jax.nn.silu(gate_proj) * up_proj).astype(jnp.bfloat16)
        down_all = w_down[expert]
        accum_sum = jnp.zeros((expert_rows, D), jnp.float32)
        for quarter_idx in range(N_SEQ):
            part_term = jnp.dot(hidden[:, quarter_idx * quarter:(quarter_idx + 1) * quarter],
                                down_all[quarter_idx * quarter:(quarter_idx + 1) * quarter],
                                preferred_element_type=jnp.float32).astype(jnp.bfloat16)
            part_term = lax.optimization_barrier(part_term)
            accum_sum = accum_sum + part_term.astype(jnp.float32)
        expert_out = accum_sum.astype(jnp.bfloat16)
        scale_rows = jnp.where(is_live, flat_weight[safe_idx], jnp.zeros((), jnp.float32))
        contribution = scale_rows[:, None] * expert_out.astype(jnp.float32)
        return combined.at[token_idx].add(contribution), None

    start_sum = jnp.zeros((TOKENS, D), jnp.float32)
    combined, unused = lax.scan(one_expert, start_sum, jnp.arange(EXPERTS, dtype=jnp.int32))
    moe_out = combined.astype(jnp.bfloat16)

    inverse = jnp.zeros((N_DEC,), jnp.int32).at[plan].set(jnp.arange(N_DEC, dtype=jnp.int32))
    handed = prefill_cache[inverse]
    lengths = prompt_len[inverse]
    position = jnp.arange(PMAX, dtype=jnp.int32)
    live_rows = position[None, :] < lengths[:, None]
    handed_cache = jnp.where(live_rows[:, :, None], handed, jnp.zeros((), prefill_cache.dtype))
    return (moe_out, handed_cache)
```

```python
import jax
import jax.numpy as jnp
from jax import lax
from jax.experimental import pallas as pl
from jax.experimental.pallas import tpu as pltpu
from jax.sharding import PartitionSpec as P

MESH = pl.DeviceIdType.MESH
AX = ("z", "x", "y")
ORDER = (("y", "x", "z"), ("z", "y", "x"), ("x", "z", "y"))
NCH = 15
NOUT = 14
LANES = 256
SLOTS = 6
bf16 = jnp.bfloat16
f32 = jnp.float32


def mod4(v):
    return lax.rem(v + 8, 4)


def kernel(
    inv_ref, xin_ref, cache_ref, wg_ref, wu_ref, wd_ref,
    fo_ref, co_ref,
    X, xr, Wgu, Wd, acc, H, wb, R, RA1, RA2, T, RB1, RB2, U, RC1, RC2, C1, C2,
    x_sem, ag_s, ag_r, ag3_s, ag3_r, agp_s, agp_r, w_sem, wd_sem,
    rp_s, rp_r, rs_s, rs_r, fo_sem, c1_s, c1_r, cp_sem, c2_s, c2_r,
):
    dec = lax.axis_index("dec")
    y = lax.axis_index("seq")
    c = lax.rem(dec, 2)
    chip = dec // 2
    me = {"z": dec // 8, "x": lax.rem(dec // 2, 4), "y": y}

    def dev(pos, core):
        return ((pos["z"] * 4 + pos["x"]) * 2 + core, pos["y"])

    def neighbour(a, d):
        pos = dict(me)
        pos[a] = mod4(me[a] + d)
        return dev(pos, c)

    partner = dev(me, 1 - c)

    def plane_id(o):
        return (lax.rem(chip + o, 16) * 2 + c, y)

    def w_copies(i, g):
        n = 3 * i + g
        slot = lax.rem(n, SLOTS)
        j = 5 * g + i
        out = []
        for h in range(2):
            half = c if h == 0 else 1 - c
            row = pl.multiple_of(half * 3584 + j * LANES, LANES)
            for m, src in enumerate((wg_ref, wu_ref)):
                out.append(pltpu.make_async_copy(
                    src.at[0, pl.ds(row, LANES), :],
                    Wgu.at[slot, pl.ds(h * LANES, LANES), pl.ds(m * 512, 512)],
                    w_sem.at[slot, 2 * h + m]))
        return out

    def wd_copies(j):
        out = []
        for h in range(2):
            half = c if h == 0 else 1 - c
            col = pl.multiple_of(half * 3584 + j * LANES, LANES)
            out.append(pltpu.make_async_copy(
                wd_ref.at[0, :, pl.ds(col, LANES)],
                Wd.at[j, :, pl.ds(h * LANES, LANES)],
                wd_sem.at[j, h]))
        return out

    for i in range(2):
        for g in range(3):
            for cp in w_copies(i, g):
                cp.start()

    barrier = pltpu.get_barrier_semaphore()
    for o in range(1, 16):
        pl.semaphore_signal(barrier, inc=1, device_id=plane_id(o), device_id_type=MESH)
    for d in (1, -1):
        pl.semaphore_signal(barrier, inc=1, device_id=neighbour("y", d), device_id_type=MESH)
    pl.semaphore_signal(barrier, inc=1, device_id=partner, device_id_type=MESH)
    pl.semaphore_wait(barrier, 18)

    swap = pltpu.make_async_remote_copy(
        xin_ref.at[1 - c], xr, x_sem.at[0], x_sem.at[1], device_id=partner, device_id_type=MESH)
    swap.start()

    def wd_start(j, _):
        for cp in wd_copies(j):
            cp.start()
        return 0

    lax.fori_loop(0, NOUT, wd_start, 0)
    swap.wait()
    for j in range(NCH):
        lane = slice(j * LANES, (j + 1) * LANES)
        X[j, me["z"], me["x"], me["y"], :, 0:LANES] = xin_ref[c, :, lane] + xr[:, lane]

    def ag_copy(g, stage, kind, i=0):
        a = ORDER[g][stage]
        done = [b for b in AX if b in ORDER[g][:stage]]
        spec = {b: (slice(None) if b in done else me[b]) for b in AX}
        spec[a] = mod4(me[a] + (0, 0, -1, 1)[kind])
        lanes = pl.ds(0, LANES)
        if kind >= 2:
            if stage == 0:
                lanes = pl.ds((kind - 2) * 128, 128)
            else:
                spec[done[0]] = pl.ds((kind - 2) * 2, 2)
        if stage < 2:
            rows, s, r = pl.ds(5 * g, 5), ag_s.at[stage, g, kind], ag_r.at[stage, g, kind]
        else:
            j = 5 * g + i
            rows, s, r = j, ag3_s.at[j, kind], ag3_r.at[j, kind]
        ref = X.at[rows, spec["z"], spec["x"], spec["y"], :, lanes]
        return pltpu.make_async_remote_copy(
            ref, ref, s, r, device_id=neighbour(a, 1 if kind % 2 == 0 else -1), device_id_type=MESH)

    def ag_partner(j):
        return pltpu.make_async_remote_copy(
            X.at[j, :, :, :, :, pl.ds(0, LANES)], X.at[j, :, :, :, :, pl.ds(LANES, LANES)],
            agp_s.at[j], agp_r.at[j], device_id=partner, device_id_type=MESH)

    def c1_copy(o):
        to = lax.rem(chip + o, 16)
        return pltpu.make_async_remote_copy(
            cache_ref.at[to], C1.at[chip], c1_s.at[o], c1_r.at[o],
            device_id=plane_id(o), device_id_type=MESH)

    def c2_copy(o):
        to = lax.rem(chip + o, 16)
        return pltpu.make_async_remote_copy(
            C2.at[to], co_ref.at[chip], c2_s.at[o], c2_r.at[o],
            device_id=plane_id(o), device_id_type=MESH)

    for stage in range(2):
        for g in range(3):
            for kind in range(2):
                ag_copy(g, stage, kind).start()
        if stage == 1:
            def c1_start(o, _):
                c1_copy(o).start()
                return 0

            lax.fori_loop(1, 16, c1_start, 0)
            C1[chip] = cache_ref[chip]
            acc[...] = jnp.zeros_like(acc)
        for g in range(3):
            for kind in range(2):
                ag_copy(g, stage, kind).wait_recv()
                ag_copy(g, stage, kind + 2).start()
        for g in range(3):
            for kind in range(2):
                ag_copy(g, stage, kind + 2).wait_recv()

    def ag3_start(i, _):
        for g in range(3):
            for kind in range(2):
                ag_copy(g, 2, kind, i).start()
        return 0

    lax.fori_loop(0, 5, ag3_start, 0)

    def valid(i, g, top=5):
        return (i >= 0) & (i < (4 if g == 2 else top))

    def gate_up(i, g):
        j = 5 * g + i
        slot = lax.rem(3 * i + g, SLOTS)
        for cp in w_copies(i, g):
            cp.wait()

        def rows(zi, _):
            xb = X[j, zi].reshape(256, 512)
            acc[zi] += jnp.dot(xb, Wgu[slot], preferred_element_type=f32)
            return 0

        lax.fori_loop(0, 4, rows, 0)

        @pl.when(valid(i + 2, g))
        def _():
            for cp in w_copies(i + 2, g):
                cp.start()

    def ag_step(i, _):
        for g in range(3):
            @pl.when(i < 5)
            def _():
                for kind in range(2):
                    ag_copy(g, 2, kind, i).wait_recv()
                    ag_copy(g, 2, kind + 2, i).start()
        for g in range(3):
            @pl.when((i >= 1) & (i < 6))
            def _():
                for kind in range(2):
                    ag_copy(g, 2, kind + 2, i - 1).wait_recv()

            @pl.when(valid(i - 1, g))
            def _():
                ag_partner(5 * g + i - 1).start()
        for g in range(3):
            @pl.when(valid(i - 2, g))
            def _():
                ag_partner(5 * g + i - 2).wait_recv()
                gate_up(i - 2, g)

        @pl.when(i == 3)
        def _():
            def c1_wait(o, _):
                c1_copy(o).wait_recv()
                return 0

            lax.fori_loop(1, 16, c1_wait, 0)
            cp_copy().start()

        return 0

    def cp_copy():
        return pltpu.make_async_remote_copy(
            C1.at[pl.ds(0, 16)], C1.at[pl.ds(16, 16)], cp_sem.at[0], cp_sem.at[1],
            device_id=partner, device_id_type=MESH)

    lax.fori_loop(0, 7, ag_step, 0)

    cp_copy().wait()

    def reorder(k, _):
        C2[k] = C1[inv_ref[k]]
        return 0

    lax.fori_loop(0, 16, reorder, 0)

    def c2_start(o, _):
        c2_copy(o).start()
        return 0

    lax.fori_loop(1, 16, c2_start, 0)
    co_ref[chip] = C2[chip]

    for g in range(3):
        for kind in range(4):
            for stage in range(2):
                ag_copy(g, stage, kind).wait_send()

    def ag_drain(i, _):
        for g in range(3):
            for kind in range(4):
                ag_copy(g, 2, kind, i).wait_send()

            @pl.when(valid(i, g))
            def _():
                ag_partner(5 * g + i).wait_send()
        return 0

    lax.fori_loop(0, 5, ag_drain, 0)

    lane_id = lax.broadcasted_iota(jnp.int32, (128, 128), 0)
    pick = jnp.where((lax.rem(lane_id, 32) == dec) & (lane_id < 96), 1.0, 0.0).astype(bf16)

    def hidden_rows(zi, _):
        gate = acc[zi, :, 0:512]
        up = acc[zi, :, 512:1024]
        H[zi] = (gate / (1.0 + jnp.exp(-gate)) * up).astype(bf16)
        wb[zi] = jnp.dot(X[14, zi, :, :, :, 0:128].reshape(256, 128), pick,
                         preferred_element_type=f32)
        return 0

    lax.fori_loop(0, 4, hidden_rows, 0)

    def rp_copy(j):
        return pltpu.make_async_remote_copy(
            X.at[j, :, :, :, :, pl.ds(LANES, LANES)], R.at[j], rp_s.at[j], rp_r.at[j],
            device_id=partner, device_id_type=MESH)

    def down(i, g):
        j = 5 * g + i
        for cp in wd_copies(j):
            cp.wait()

        def rows(zi, _):
            part = jnp.dot(H[zi], Wd[j], preferred_element_type=f32)
            w = wb[zi]
            part = part * jnp.concatenate([w, w, w, w], axis=1)
            X[j, zi] = part.astype(bf16).reshape(4, 4, 16, 512)
            return 0

        lax.fori_loop(0, 4, rows, 0)
        rp_copy(j).start()

    def chip_sum(j):
        rp_copy(j).wait_recv()

        def rows(zi, _):
            own = X[j, zi, :, :, :, 0:LANES].astype(f32)
            X[j, zi, :, :, :, 0:LANES] = (own + R[j, zi].astype(f32)).astype(bf16)
            return 0

        lax.fori_loop(0, 4, rows, 0)

    def part_of(g, stage, j, at, half=None):
        a1, a2, a3 = ORDER[g]
        hs = slice(None) if half is None else pl.ds(2 * half, 2)
        if stage == 0:
            spec = {b: slice(None) for b in AX}
            rest = [b for b in AX if b != a3]
            spec[a3], spec[rest[0]] = at, hs
            return X.at[j, spec["z"], spec["x"], spec["y"], :, pl.ds(0, LANES)]
        if stage == 1:
            rest = [b for b in AX if b != a3]
            if rest[0] == a2:
                return T.at[j, at, hs]
            return T.at[j, hs, at]
        if half is None:
            return U.at[j, at]
        return U.at[j, at, :, pl.ds(128 * half, 128)]

    first = (RA1, RB1, RC1)
    second = (RA2, RB2, RC2)
    result = (T, U, fo_ref.at[0])

    def rs_copy(g, stage, kind, j):
        a = ORDER[g][2 - stage]
        p = me[a]
        if kind < 2:
            src, dst = part_of(g, stage, j, mod4(p + 2), kind), first[stage].at[kind, j]
        else:
            src = part_of(g, stage, j, mod4(p + (1 if kind == 2 else -1)))
            dst = second[stage].at[kind - 2, j]
        return pltpu.make_async_remote_copy(
            src, dst, rs_s.at[j, stage, kind], rs_r.at[j, stage, kind],
            device_id=neighbour(a, 1 if kind % 2 == 0 else -1), device_id_type=MESH)

    def rs_first(g, stage, j):
        for kind in range(2):
            rs_copy(g, stage, kind, j).start()

    def rs_second(g, stage, j):
        p = me[ORDER[g][2 - stage]]
        for kind in range(2):
            rs_copy(g, stage, kind, j).wait_recv()
            ref = part_of(g, stage, j, mod4(p + (1 if kind == 0 else -1)), kind)
            ref[...] = (ref[...].astype(f32) + first[stage][kind, j].astype(f32)).astype(bf16)
            rs_copy(g, stage, kind + 2, j).start()

    def rs_last(g, stage, j):
        p = me[ORDER[g][2 - stage]]
        for kind in range(2):
            rs_copy(g, stage, kind + 2, j).wait_recv()
        total = (part_of(g, stage, j, p)[...].astype(f32) + second[stage][0, j].astype(f32)
                 + second[stage][1, j].astype(f32))
        result[stage][j] = total.astype(bf16)

    def rs_step(i, _):
        for g in range(3):
            @pl.when(valid(i, g))
            def _():
                down(i, g)
        for g in range(3):
            @pl.when(valid(i, g))
            def _():
                chip_sum(5 * g + i)
                rs_first(g, 0, 5 * g + i)
        for stage in range(3):
            lag = 1 + 2 * stage
            for g in range(3):
                @pl.when(valid(i - lag, g))
                def _():
                    rs_second(g, stage, 5 * g + i - lag)
            for g in range(3):
                @pl.when(valid(i - lag - 1, g))
                def _():
                    rs_last(g, stage, 5 * g + i - lag - 1)
                    if stage < 2:
                        rs_first(g, stage + 1, 5 * g + i - lag - 1)
        return 0

    lax.fori_loop(0, 11, rs_step, 0)

    fo = pltpu.make_async_remote_copy(
        fo_ref.at[0], fo_ref.at[1], fo_sem.at[0], fo_sem.at[1],
        device_id=partner, device_id_type=MESH)
    fo.start()

    def c_drain(o, _):
        c1_copy(o).wait_send()
        c2_copy(o).wait()
        return 0

    lax.fori_loop(1, 16, c_drain, 0)

    def rs_drain(i, _):
        for g in range(3):
            @pl.when(valid(i, g))
            def _():
                j = 5 * g + i
                rp_copy(j).wait_send()
                for stage in range(3):
                    for kind in range(4):
                        rs_copy(g, stage, kind, j).wait_send()
        return 0

    lax.fori_loop(0, 5, rs_drain, 0)
    fo.wait()


def body(
    hidden_states, gate_scores, expert_ids, w_gate, w_up, w_down, prefill_cache, plan, prompt_len
):
    dec = lax.axis_index("dec")
    seq = lax.axis_index("seq")
    core = lax.rem(dec, 2)
    n_dec = 32

    affinity = jax.nn.sigmoid(gate_scores)
    weight = 2.5 * affinity / jnp.sum(affinity, axis=1, keepdims=True)
    experts = jnp.arange(n_dec, dtype=jnp.int32)
    dense = jnp.sum(
        jnp.where(expert_ids[:, :, None] == experts[None, None, :], weight[:, :, None], 0.0), axis=1)
    hi = lax.reduce_precision(dense, 8, 7)
    mid = lax.reduce_precision(dense - hi, 8, 7)
    low = dense - hi - mid
    zeros = jnp.zeros((8, 160), f32)
    extra = jnp.concatenate([hi, mid, low, zeros], axis=1).astype(bf16)
    halves = jnp.stack([
        jnp.concatenate([hidden_states[:, :3584], extra], axis=1),
        jnp.concatenate([hidden_states[:, 3584:], extra], axis=1)])
    both = jnp.concatenate([halves, halves], axis=1)
    mine = lax.broadcasted_iota(jnp.int32, both.shape, 1) // 8 == core
    xin = jnp.where(mine, both, jnp.zeros((), bf16))

    indices = jnp.arange(n_dec, dtype=jnp.int32)
    inverse = jnp.sum(jnp.where(plan[None, :] == indices[:, None], indices[None, :], 0), axis=1)
    length = jnp.sum(jnp.where(plan == dec, prompt_len, 0))
    of_core = jnp.where(core == 0, inverse[0::2], inverse[1::2])
    order = lax.rem(lax.rem(of_core, 2) + core, 2) * 16 + of_core // 2

    vm = pl.BlockSpec(memory_space=pltpu.VMEM)
    hbm = pl.BlockSpec(memory_space=pl.ANY)
    dma = pltpu.SemaphoreType.DMA
    fo, co = pl.pallas_call(
        kernel,
        out_shape=(
            jax.ShapeDtypeStruct((2, NOUT, 16, LANES), bf16),
            jax.ShapeDtypeStruct((16, 16, 576), bf16),
        ),
        in_specs=[pl.BlockSpec(memory_space=pltpu.SMEM), vm, vm, hbm, hbm, hbm],
        out_specs=(vm, vm),
        scratch_shapes=[
            pltpu.VMEM((NCH, 4, 4, 4, 16, 512), bf16),
            pltpu.VMEM((16, NCH * LANES), bf16),
            pltpu.VMEM((SLOTS, 512, 1024), bf16),
            pltpu.VMEM((NOUT, 512, 512), bf16),
            pltpu.VMEM((4, 256, 1024), f32),
            pltpu.VMEM((4, 256, 512), bf16),
            pltpu.VMEM((4, 256, 128), f32),
            pltpu.VMEM((NOUT, 4, 4, 4, 16, LANES), bf16),
            pltpu.VMEM((2, NOUT, 2, 4, 16, LANES), bf16),
            pltpu.VMEM((2, NOUT, 4, 4, 16, LANES), bf16),
            pltpu.VMEM((NOUT, 4, 4, 16, LANES), bf16),
            pltpu.VMEM((2, NOUT, 2, 16, LANES), bf16),
            pltpu.VMEM((2, NOUT, 4, 16, LANES), bf16),
            pltpu.VMEM((NOUT, 4, 16, LANES), bf16),
            pltpu.VMEM((2, NOUT, 16, 128), bf16),
            pltpu.VMEM((2, NOUT, 16, LANES), bf16),
            pltpu.VMEM((32, 16, 576), bf16),
            pltpu.VMEM((16, 16, 576), bf16),
            dma((2,)),
            dma((2, 3, 4)), dma((2, 3, 4)),
            dma((NCH, 4)), dma((NCH, 4)),
            dma((NCH,)), dma((NCH,)),
            dma((SLOTS, 4)), dma((NOUT, 2)),
            dma((NOUT,)), dma((NOUT,)),
            dma((NOUT, 3, 4)), dma((NOUT, 3, 4)),
            dma((2,)),
            dma((16,)), dma((16,)),
            dma((2,)),
            dma((16,)), dma((16,)),
        ],
        compiler_params=pltpu.CompilerParams(
            collective_id=0, has_side_effects=True, vmem_limit_bytes=60 * 1024 * 1024),
        cost_estimate=pl.CostEstimate(
            flops=22_500_000_000, bytes_accessed=23_000_000, transcendentals=524288),
    )(order, xin, prefill_cache.reshape(16, 16, 576), w_gate, w_up, w_down)

    rows = jnp.where(core == 0, fo[:, :, :8], fo[:, :, 8:])
    rows = jnp.transpose(rows, (2, 0, 1, 3)).reshape(8, 2, 3584)
    moe_out = jnp.where(core == 0, rows, rows[:, ::-1]).reshape(8, 7168)

    position = seq * 256 + jnp.arange(256, dtype=jnp.int32)
    handed = co.reshape(1, 256, 576)
    handed_cache = jnp.where((position < length)[None, :, None], handed, jnp.zeros((), bf16))
    return (moe_out, handed_cache)


def solution(mesh):
    in_specs = (
        P(("dec", "seq"), None),
        P(("dec", "seq"), None),
        P(("dec", "seq"), None),
        P("dec", None, "seq"),
        P("dec", None, "seq"),
        P("dec", "seq", None),
        P("dec", "seq", None),
        P(),
        P(),
    )
    out_specs = (P(("dec", "seq"), None), P("dec", "seq", None))
    return jax.shard_map(body, mesh=mesh, in_specs=in_specs, out_specs=out_specs, check_vma=False)
```

```python
import jax
import jax.numpy as jnp
from jax import lax
from jax.experimental import pallas as pl
from jax.experimental.pallas import tpu as pltpu
from jax.sharding import PartitionSpec as P

MESH = pl.DeviceIdType.MESH
AX = ("z", "x", "y")
ORDER = (("y", "x", "z"), ("z", "y", "x"), ("x", "z", "y"))
NCH = 15
NOUT = 14
LANES = 256
HALF = NOUT * LANES
SLOTS = 6
PIECES = 12
bf16 = jnp.bfloat16
f32 = jnp.float32


def mod4(v):
    return lax.rem(v + 8, 4)


def loop(lo, hi, fn):
    def step(k, carry):
        fn(k)
        return carry

    lax.fori_loop(lo, hi, step, 0)


def kernel(
    plan_hbm, plen_hbm, scores_hbm, ids_hbm, hid_hbm, cache_ref, wg_ref, wu_ref, wd_ref,
    moe_hbm, co_hbm,
    X, xin, xr, Wgu, Wd, acc, H, wb, R, RA1, RA2, T, RB, U, RC, FS, FR, C1, C2, order_ref,
    plan_ref, plen_ref, scores_ref, ids_ref, hid_ref, moe_ref, co_ref, io_sem,
    x_sem, ag_s, ag_r, ag3_s, ag3_r, agp_s, agp_r, w_sem, wd_sem,
    rp_s, rp_r, rs_s, rs_r, rb_s, rb_r, fo_sem, c_sem, cp_sem,
):
    dec = lax.axis_index("dec")
    y = lax.axis_index("seq")
    c = lax.rem(dec, 2)
    chip = dec // 2
    me = {"z": dec // 8, "x": lax.rem(dec // 2, 4), "y": y}

    def dev(pos, core):
        return ((pos["z"] * 4 + pos["x"]) * 2 + core, pos["y"])

    def peer(a, d):
        pos = dict(me)
        pos[a] = mod4(me[a] + d)
        return dev(pos, c)

    partner = dev(me, 1 - c)

    def plane_id(o):
        return (lax.rem(chip + o, 16) * 2 + c, y)

    def remote(src, dst, s, r, to):
        return pltpu.make_async_remote_copy(src, dst, s, r, device_id=to, device_id_type=MESH)

    loads = [pltpu.make_async_copy(src, dst, io_sem.at[q]) for q, (src, dst) in enumerate((
        (hid_hbm, hid_ref), (scores_hbm, scores_ref), (ids_hbm, ids_ref),
        (plan_hbm, plan_ref), (plen_hbm, plen_ref)))]
    for cp in loads:
        cp.start()

    def take(sem, ref):
        pltpu.make_async_copy(ref, ref, sem).wait()

    barrier = pltpu.get_barrier_semaphore()
    for o in range(1, 16):
        pl.semaphore_signal(barrier, inc=1, device_id=plane_id(o), device_id_type=MESH)
    for d in (1, -1, 2):
        pl.semaphore_signal(barrier, inc=1, device_id=peer("y", d), device_id_type=MESH)
    pl.semaphore_signal(barrier, inc=1, device_id=partner, device_id_type=MESH)

    def w_copies(i, g):
        slot = lax.rem(3 * i + g, SLOTS)
        j = 5 * g + i
        out = []
        for h in range(2):
            half = c if h == 0 else 1 - c
            row = pl.multiple_of(half * HALF + j * LANES, LANES)
            for m, src in enumerate((wg_ref, wu_ref)):
                out.append(pltpu.make_async_copy(
                    src.at[0, pl.ds(row, LANES), :],
                    Wgu.at[slot, pl.ds(h * LANES, LANES), pl.ds(m * 512, 512)],
                    w_sem.at[slot]))
        return out

    def wd_copies(j):
        out = []
        for h in range(2):
            half = c if h == 0 else 1 - c
            col = pl.multiple_of(half * HALF + j * LANES, LANES)
            out.append(pltpu.make_async_copy(
                wd_ref.at[0, :, pl.ds(col, LANES)],
                Wd.at[j, :, pl.ds(h * LANES, LANES)],
                wd_sem.at[j]))
        return out

    for i in range(2):
        for g in range(3):
            for cp in w_copies(i, g):
                cp.start()

    for cp in loads:
        cp.wait()
    score = 1.0 / (1.0 + jnp.exp(-scores_ref[...]))
    weight = 2.5 * score / jnp.sum(score, axis=1, keepdims=True)
    ids = ids_ref[...]
    lane8 = lax.broadcasted_iota(jnp.int32, (8, 128), 1)
    dense = jnp.zeros((8, 128), f32)
    for k in range(8):
        dense += jnp.where(ids[:, k:k + 1] == lane8 % 32, weight[:, k:k + 1], 0.0)
    hi = dense.astype(bf16).astype(f32)
    mid = (dense - hi).astype(bf16).astype(f32)
    low = dense - hi - mid
    part = lane8 // 32
    extra = jnp.where(part == 0, hi, jnp.where(part == 1, mid, jnp.where(part == 2, low, 0.0)))

    def two(v):
        mine = lax.broadcasted_iota(jnp.int32, (16, v.shape[1]), 0) // 8 == c
        return jnp.where(mine, jnp.concatenate([v, v], axis=0), 0.0).astype(bf16)

    for h in range(2):
        for t in range(NOUT):
            lane = slice(h * HALF + t * LANES, h * HALF + (t + 1) * LANES)
            xin[h, :, t * LANES:(t + 1) * LANES] = two(hid_ref[:, lane].astype(f32))
        xin[h, :, HALF:HALF + 128] = two(extra)
        xin[h, :, HALF + 128:HALF + 256] = jnp.zeros((16, 128), bf16)

    pl.semaphore_wait(barrier, 19)

    swap = remote(xin.at[1 - c], xr, x_sem.at[0], x_sem.at[1], partner)
    swap.start()
    swap.wait()
    for j in range(NCH):
        lane = slice(j * LANES, (j + 1) * LANES)
        X[j, me["z"], me["x"], me["y"], :, 0:LANES] = xin[c, :, lane] + xr[:, lane]

    PEERS = (1, -1, 2)

    def ag_copy(g, stage, part, q):
        a = ORDER[g][stage]
        done = ORDER[g][:stage]
        spec = {b: (slice(None) if b in done else me[b]) for b in AX}
        rows = pl.ds(5 * g, 1) if part == 0 else pl.ds(5 * g + 1, 4)
        ref = X.at[rows, spec["z"], spec["x"], spec["y"], :, pl.ds(0, LANES)]
        return remote(ref, ref, ag_s.at[stage], ag_r.at[stage, part],
                      peer(a, PEERS[q]))

    def ag3_copy(g, kind, i):
        a = ORDER[g][2]
        done = [b for b in AX if b != a]
        spec = {b: slice(None) for b in AX}
        spec[a] = mod4(me[a] + (0, 0, -1, 1)[kind])
        if kind >= 2:
            spec[done[0]] = pl.ds((kind - 2) * 2, 2)
        j = 5 * g + i
        ref = X.at[j, spec["z"], spec["x"], spec["y"], :, pl.ds(0, LANES)]
        return remote(ref, ref, ag3_s, ag3_r.at[j, kind // 2],
                      peer(a, 1 if kind % 2 == 0 else -1))

    def ag_partner(j):
        return remote(
            X.at[j, :, :, :, :, pl.ds(0, LANES)], X.at[j, :, :, :, :, pl.ds(LANES, LANES)],
            agp_s, agp_r.at[j], partner)

    def piece(k):
        return pl.ds(pl.multiple_of(k * 48, 16), 48)

    serves = chip < PIECES

    def c1_copy(o):
        to = lax.rem(chip + o, 16)
        return remote(cache_ref.at[0, piece(to), :], C1.at[chip], c_sem.at[0], c_sem.at[1],
                      plane_id(o))

    def c2_copy(o):
        to = lax.rem(chip + o, 16)
        return remote(C2.at[to], co_ref.at[piece(chip), :], c_sem.at[2], c_sem.at[3],
                      plane_id(o))

    def cp_copy():
        return remote(C1.at[pl.ds(0, 16)], C1.at[pl.ds(16, 16)], cp_sem.at[0], cp_sem.at[1],
                      partner)

    def ag_all(stage, part, act):
        for g in range(3):
            for q in range(3):
                act(ag_copy(g, stage, part, q))

    def start(cp):
        cp.start()

    def ag_take(stage, part):
        ref = X.at[pl.ds(0, 9), 0, pl.ds(0, 4 ** part), pl.ds(0, 4 ** stage), :, pl.ds(0, LANES)]
        take(ag_r.at[stage, part], ref)

    def ag3_take(i, g, k):
        a = ORDER[g][2]
        spec = {b: slice(None) for b in AX}
        spec[a] = pl.ds(0, 2 - k)
        take(ag3_r.at[5 * g + i, k],
             X.at[5 * g + i, spec["z"], spec["x"], spec["y"], :, pl.ds(0, LANES)])

    ag_all(0, 0, start)
    ag_all(0, 1, start)

    def wd_start(j):
        for cp in wd_copies(j):
            cp.start()

    loop(0, NOUT, wd_start)
    acc[...] = jnp.zeros_like(acc)

    def find(k):
        d = 2 * k + c
        src = jnp.int32(0)
        for q in range(32):
            src = jnp.where(plan_ref[q] == d, jnp.int32(q), src)
        order_ref[k] = lax.rem(lax.rem(src, 2) + c, 2) * 16 + src // 2

    ag_take(0, 0)
    ag_all(1, 0, start)
    ag_take(0, 1)
    ag_all(1, 1, start)

    def c1_own():
        return pltpu.make_async_copy(cache_ref.at[0, piece(chip), :], C1.at[chip], c_sem.at[4])

    def c1_start(o):
        @pl.when(lax.rem(chip + o, 16) < PIECES)
        def _():
            c1_copy(o).start()

    loop(1, 16, c1_start)

    @pl.when(serves)
    def _():
        c1_own().start()

    loop(0, 16, find)

    def ag3_start(i):
        for g in range(3):
            for kind in range(2):
                ag3_copy(g, kind, i).start()

    ag_take(1, 0)
    ag3_start(0)
    ag_take(1, 1)
    ag3_start(1)

    def valid(i, g):
        return (i >= 0) & (i < (4 if g == 2 else 5))

    def gate_up(i, g):
        j = 5 * g + i
        slot = lax.rem(3 * i + g, SLOTS)
        take(w_sem.at[slot], Wgu.at[slot])

        for zi in range(4):
            xb = X[j, zi].reshape(256, 512)
            acc[zi] += jnp.dot(xb, Wgu[slot], preferred_element_type=f32)

        @pl.when(valid(i + 2, g))
        def _():
            for cp in w_copies(i + 2, g):
                cp.start()

    def ag_step(i):
        for g in range(3):
            @pl.when(i < 5)
            def _():
                ag3_take(i, g, 0)
                for kind in range(2):
                    ag3_copy(g, kind + 2, i).start()

            @pl.when(i + 2 < 5)
            def _():
                for kind in range(2):
                    ag3_copy(g, kind, i + 2).start()

            @pl.when(valid(i - 2, g))
            def _():
                ag_partner(5 * g + i - 2).wait_recv()
                gate_up(i - 2, g)

            @pl.when((i >= 1) & (i < 6))
            def _():
                ag3_take(i - 1, g, 1)

            @pl.when(valid(i - 1, g))
            def _():
                ag_partner(5 * g + i - 1).start()

        @pl.when(i == 2)
        def _():
            @pl.when(serves)
            def _():
                take(c_sem.at[1], C1.at[pl.ds(0, 15)])
                c1_own().wait()
                cp_copy().start()

        @pl.when(i == 5)
        def _():
            @pl.when(serves)
            def _():
                cp_copy().wait()

                def reorder(k):
                    C2[k] = C1[order_ref[k]]

                loop(0, 16, reorder)
                loop(1, 16, lambda o: c2_copy(o).start())
                co_ref[piece(chip), :] = C2[chip]

    loop(0, 7, ag_step)

    low_lanes = pl.ds(0, LANES)
    take(ag_s.at[0], X.at[:, 0, 0, pl.ds(0, 3), :, low_lanes])
    take(ag_s.at[1], X.at[:, 0, pl.ds(0, 3), :, :, low_lanes])
    take(ag3_s, X.at[:, pl.ds(0, 3), :, :, :, low_lanes])
    take(agp_s, X.at[pl.ds(0, NOUT), :, :, :, :, low_lanes])

    lane_id = lax.broadcasted_iota(jnp.int32, (128, 128), 0)
    pick = jnp.where((lax.rem(lane_id, 32) == dec) & (lane_id < 96), 1.0, 0.0).astype(bf16)

    def hidden_rows(zi):
        gate = acc[zi, :, 0:512]
        up = acc[zi, :, 512:1024]
        H[zi] = (gate / (1.0 + jnp.exp(-gate)) * up).astype(bf16)
        wb[zi] = jnp.dot(X[14, zi, :, :, :, 0:128].reshape(256, 128), pick,
                         preferred_element_type=f32)

    loop(0, 4, hidden_rows)

    def rp_copy(j):
        return remote(X.at[j, :, :, :, :, pl.ds(LANES, LANES)], R.at[j], rp_s, rp_r.at[j],
                      partner)

    def down(i, g):
        j = 5 * g + i
        take(wd_sem.at[j], Wd.at[j])

        for zi in range(4):
            out = jnp.dot(H[zi], Wd[j], preferred_element_type=f32)
            w = wb[zi]
            out = out * jnp.concatenate([w, w, w, w], axis=1)
            X[j, zi] = out.astype(bf16).reshape(4, 4, 16, 512)
        rp_copy(j).start()

    def chip_sum(j):
        rp_copy(j).wait_recv()

        def rows(zi):
            X[j, zi, :, :, :, 0:LANES] += R[j, zi]

        loop(0, 4, rows)

    def plane_of(g, j, at, half=None):
        a = ORDER[g][2]
        rest = [b for b in AX if b != a]
        spec = {b: slice(None) for b in AX}
        spec[a] = at
        if half is not None:
            spec[rest[0]] = pl.ds(2 * half, 2)
        return X.at[j, spec["z"], spec["x"], spec["y"], :, pl.ds(0, LANES)]

    def rs_copy(g, kind, j):
        a = ORDER[g][2]
        p = me[a]
        if kind < 2:
            src, dst = plane_of(g, j, mod4(p + 2), kind), RA1.at[kind, j]
        else:
            src, dst = plane_of(g, j, mod4(p + (1 if kind == 2 else -1))), RA2.at[kind - 2, j]
        return remote(src, dst, rs_s.at[kind // 2], rs_r.at[j, kind // 2],
                      peer(a, 1 if kind % 2 == 0 else -1))

    def line_of(g, stage, j, at):
        if stage == 0:
            rest = [b for b in AX if b != ORDER[g][2]]
            return T.at[j, at] if rest[0] == ORDER[g][1] else T.at[j, :, at]
        return U.at[j, at]

    def rb_copy(g, stage, q, j):
        a = ORDER[g][1 - stage]
        src = line_of(g, stage, j, mod4(me[a] + PEERS[q]))
        return remote(src, (RB, RC)[stage].at[q, j], rb_s.at[stage], rb_r.at[j, stage],
                      peer(a, PEERS[q]))

    def rs_first(g, j):
        for kind in range(2):
            rs_copy(g, kind, j).start()

    def rs_second(g, j):
        p = me[ORDER[g][2]]
        take(rs_r.at[j, 0], RA1.at[:, j])
        for kind in range(2):
            ref = plane_of(g, j, mod4(p + (1 if kind == 0 else -1)), kind)
            ref[...] += RA1[kind, j]
            rs_copy(g, kind + 2, j).start()

    def rs_last(g, j):
        take(rs_r.at[j, 1], RA2.at[:, j])
        total = (plane_of(g, j, me[ORDER[g][2]])[...].astype(f32) + RA2[0, j].astype(f32)
                 + RA2[1, j].astype(f32))
        T[j] = total.astype(bf16)

    def rb_start(g, stage, j):
        for q in range(3):
            rb_copy(g, stage, q, j).start()

    def rb_last(g, stage, j):
        buf = (RB, RC)[stage]
        take(rb_r.at[j, stage], buf.at[:, j])
        total = line_of(g, stage, j, me[ORDER[g][1 - stage]])[...].astype(f32)
        for q in range(3):
            total = total + buf[q, j].astype(f32)
        if stage == 0:
            U[j] = total.astype(bf16)
            return
        first = c == 0
        mine = jnp.where(first, total[0:8], total[8:16])
        FS[j] = jnp.where(first, total[8:16], total[0:8])
        moe_ref[:, pl.ds(pl.multiple_of(c * HALF + j * LANES, LANES), LANES)] = mine.astype(bf16)

    def co_out():
        return pltpu.make_async_copy(co_ref, co_hbm.at[0], io_sem.at[5])

    def hand_over():
        length = jnp.int32(0)
        for q in range(32):
            length = jnp.where(plan_ref[q] == dec, plen_ref[q], length)

        @pl.when(serves)
        def _():
            take(c_sem.at[3], C2.at[pl.ds(0, PIECES - 1)])

        @pl.when(jnp.logical_not(serves))
        def _():
            take(c_sem.at[3], C2.at[pl.ds(0, PIECES)])


        def mask_rows(k):
            pos = y * 256 + lax.broadcasted_iota(jnp.int32, (48, 256), 1)
            kept = co_ref[piece(k), :].astype(f32)
            co_ref[piece(k), :] = jnp.where(pos < length, kept, 0.0).astype(bf16)

        loop(0, PIECES, mask_rows)
        co_out().start()

    def rs_step(i):
        @pl.when(i == 4)
        def _():
            hand_over()

        for g in range(3):
            @pl.when(valid(i, g))
            def _():
                down(i, g)

            ib, gb = (i, g - 1) if g else (i - 1, 2)

            @pl.when(valid(ib, gb))
            def _():
                chip_sum(5 * gb + ib)
                rs_first(gb, 5 * gb + ib)

            @pl.when(valid(ib - 1, gb))
            def _():
                rs_second(gb, 5 * gb + ib - 1)

            @pl.when(valid(ib - 2, gb))
            def _():
                rs_last(gb, 5 * gb + ib - 2)
                rb_start(gb, 0, 5 * gb + ib - 2)

            @pl.when(valid(ib - 3, gb))
            def _():
                rb_last(gb, 0, 5 * gb + ib - 3)
                rb_start(gb, 1, 5 * gb + ib - 3)

            @pl.when(valid(ib - 4, gb))
            def _():
                rb_last(gb, 1, 5 * gb + ib - 4)

    loop(0, 10, rs_step)

    fo = remote(FS, FR, fo_sem.at[0], fo_sem.at[1], partner)
    fo.start()

    @pl.when(serves)
    def _():
        take(c_sem.at[0], C2.at[pl.ds(0, PIECES - 1)])
        take(c_sem.at[2], C2.at[pl.ds(0, 15)])

    @pl.when(jnp.logical_not(serves))
    def _():
        take(c_sem.at[0], C2.at[pl.ds(0, PIECES)])

    take(rp_s, R)
    take(rs_s.at[0], RA1)
    take(rs_s.at[1], RA2)
    take(rb_s.at[0], RB)
    take(rb_s.at[1], RC)
    fo.wait()
    for j in range(NOUT):
        moe_ref[:, pl.ds(pl.multiple_of((1 - c) * HALF + j * LANES, LANES), LANES)] = (
            FR[j].astype(bf16))
    moe_out = pltpu.make_async_copy(moe_ref, moe_hbm, io_sem.at[6])
    moe_out.start()
    co_out().wait()
    moe_out.wait()


def body(
    hidden_states, gate_scores, expert_ids, w_gate, w_up, w_down, prefill_cache, plan, prompt_len
):
    hbm = pl.BlockSpec(memory_space=pl.ANY)
    dma = pltpu.SemaphoreType.DMA
    moe, handed = pl.pallas_call(
        kernel,
        out_shape=(
            jax.ShapeDtypeStruct((8, 7168), bf16),
            jax.ShapeDtypeStruct((1, 576, 256), bf16),
        ),
        in_specs=[hbm] * 9,
        out_specs=(hbm, hbm),
        scratch_shapes=[
            pltpu.VMEM((NCH, 4, 4, 4, 16, 512), bf16),
            pltpu.VMEM((2, 16, NCH * LANES), bf16),
            pltpu.VMEM((16, NCH * LANES), bf16),
            pltpu.VMEM((SLOTS, 512, 1024), bf16),
            pltpu.VMEM((NOUT, 512, 512), bf16),
            pltpu.VMEM((4, 256, 1024), f32),
            pltpu.VMEM((4, 256, 512), bf16),
            pltpu.VMEM((4, 256, 128), f32),
            pltpu.VMEM((NOUT, 4, 4, 4, 16, LANES), bf16),
            pltpu.VMEM((2, NOUT, 2, 4, 16, LANES), bf16),
            pltpu.VMEM((2, NOUT, 4, 4, 16, LANES), bf16),
            pltpu.VMEM((NOUT, 4, 4, 16, LANES), bf16),
            pltpu.VMEM((3, NOUT, 4, 16, LANES), bf16),
            pltpu.VMEM((NOUT, 4, 16, LANES), bf16),
            pltpu.VMEM((3, NOUT, 16, LANES), bf16),
            pltpu.VMEM((NOUT, 8, LANES), f32),
            pltpu.VMEM((NOUT, 8, LANES), f32),
            pltpu.VMEM((32, 48, 256), bf16),
            pltpu.VMEM((16, 48, 256), bf16),
            pltpu.SMEM((16,), jnp.int32),
            pltpu.SMEM((32,), jnp.int32),
            pltpu.SMEM((32,), jnp.int32),
            pltpu.VMEM((8, 8), f32),
            pltpu.VMEM((8, 8), jnp.int32),
            pltpu.VMEM((8, 7168), bf16),
            pltpu.VMEM((8, 7168), bf16),
            pltpu.VMEM((576, 256), bf16),
            dma((7,)),
            dma((2,)),
            dma((2,)), dma((2, 2)),
            dma, dma((NCH, 2)),
            dma, dma((NOUT,)),
            dma((SLOTS,)), dma((NOUT,)),
            dma, dma((NOUT,)),
            dma((2,)), dma((NOUT, 2)),
            dma((2,)), dma((NOUT, 2)),
            dma((2,)),
            dma((5,)),
            dma((2,)),
        ],
        compiler_params=pltpu.CompilerParams(
            collective_id=0, has_side_effects=True, vmem_limit_bytes=60 * 1024 * 1024),
        cost_estimate=pl.CostEstimate(
            flops=22_500_000_000, bytes_accessed=23_000_000, transcendentals=524288),
    )(plan, prompt_len, gate_scores, expert_ids, hidden_states,
      jnp.swapaxes(prefill_cache, 1, 2), w_gate, w_up, w_down)

    def hand_on(moe_in, handed_in, moe_out, handed_out):
        moe_out[...] = moe_in[...]
        handed_out[...] = handed_in[...]

    vm = pl.BlockSpec(memory_space=pltpu.VMEM)
    moe, handed = pl.pallas_call(
        hand_on,
        out_shape=(
            jax.ShapeDtypeStruct((8, 7168), bf16),
            jax.ShapeDtypeStruct((1, 576, 256), bf16),
        ),
        in_specs=[vm, vm],
        out_specs=(vm, vm),
        cost_estimate=pl.CostEstimate(flops=0, bytes_accessed=820_000, transcendentals=0),
    )(moe, handed)
    return moe, jnp.swapaxes(handed, 1, 2)


def solution(mesh):
    in_specs = (
        P(("dec", "seq"), None),
        P(("dec", "seq"), None),
        P(("dec", "seq"), None),
        P("dec", None, "seq"),
        P("dec", None, "seq"),
        P("dec", "seq", None),
        P("dec", "seq", None),
        P(),
        P(),
    )
    out_specs = (P(("dec", "seq"), None), P("dec", "seq", None))
    return jax.shard_map(body, mesh=mesh, in_specs=in_specs, out_specs=out_specs, check_vma=False)
```

```python
import jax
import jax.numpy as jnp
from jax import lax
from jax.experimental import pallas as pl
from jax.experimental.pallas import tpu as pltpu
from jax.sharding import PartitionSpec as P

MESH = pl.DeviceIdType.MESH
AX = ("z", "x", "y")
ORDER = (("y", "x", "z"), ("z", "y", "x"), ("x", "z", "y"))
NCH = 15
NOUT = 14
LANES = 256
HALF = NOUT * LANES
SLOTS = 6
PIECES = 12
bf16 = jnp.bfloat16
f32 = jnp.float32


def mod4(v):
    return lax.rem(v + 8, 4)


def loop(lo, hi, fn):
    def step(k, carry):
        fn(k)
        return carry

    lax.fori_loop(lo, hi, step, 0)


def kernel(
    plan_hbm, plen_hbm, scores_hbm, ids_hbm, hid_hbm, cache_ref, wg_ref, wu_ref, wd_ref,
    moe_hbm, co_hbm,
    X, xin, xr, ext, extr, Wgu, Wd, acc, H, wb, R, RA1, RA2, T, RB, U, RC, RT, FS, FR, C1, C2, order_ref,
    plan_ref, plen_ref, scores_ref, ids_ref, hid_ref, moe_ref, co_ref, io_sem,
    x_sem, ag_s, ag_r, ag3_s, ag3_r, agp_s, agp_r, w_sem, wd_sem,
    rp_s, rp_r, rs_s, rs_r, rb_s, rb_r, rt_s, rt_r, fo_sem, c_sem, cp_sem,
):
    dec = lax.axis_index("dec")
    y = lax.axis_index("seq")
    c = lax.rem(dec, 2)
    chip = dec // 2
    me = {"z": dec // 8, "x": lax.rem(dec // 2, 4), "y": y}

    def dev(pos, core):
        return ((pos["z"] * 4 + pos["x"]) * 2 + core, pos["y"])

    def peer(a, d):
        pos = dict(me)
        pos[a] = mod4(me[a] + d)
        return dev(pos, c)

    def mate(a, b, o):
        pos = dict(me)
        pos[a] = mod4(me[a] + o // 4)
        pos[b] = mod4(me[b] + o % 4)
        return dev(pos, c)

    partner = dev(me, 1 - c)

    def plane_id(o):
        return (lax.rem(chip + o, 16) * 2 + c, y)

    def remote(src, dst, s, r, to):
        return pltpu.make_async_remote_copy(src, dst, s, r, device_id=to, device_id_type=MESH)

    loads = [pltpu.make_async_copy(src, dst, io_sem.at[q]) for q, (src, dst) in enumerate((
        (hid_hbm, hid_ref), (scores_hbm, scores_ref), (ids_hbm, ids_ref),
        (plan_hbm, plan_ref), (plen_hbm, plen_ref)))]
    for cp in loads:
        cp.start()

    def take(sem, ref):
        pltpu.make_async_copy(ref, ref, sem).wait()

    barrier = pltpu.get_barrier_semaphore()
    for o in range(1, 16):
        pl.semaphore_signal(barrier, inc=1, device_id=plane_id(o), device_id_type=MESH)
    for o in range(4, 16):
        pl.semaphore_signal(barrier, inc=1, device_id=mate("y", "x", o), device_id_type=MESH)
    for o in range(5, 16):
        if o % 4:
            pl.semaphore_signal(barrier, inc=1, device_id=mate("z", "y", o), device_id_type=MESH)
    pl.semaphore_signal(barrier, inc=1, device_id=partner, device_id_type=MESH)

    def piece(k):
        return pl.ds(pl.multiple_of(k * 48, 16), 48)

    serves = chip < PIECES

    def c1_copy(o):
        to = lax.rem(chip + o, 16)
        return remote(cache_ref.at[0, piece(to), :], C1.at[chip], c_sem.at[0], c_sem.at[1],
                      plane_id(o))

    def c2_copy(o):
        to = lax.rem(chip + o, 16)
        return remote(C2.at[to], co_ref.at[piece(chip), :], c_sem.at[2], c_sem.at[3],
                      plane_id(o))

    def cp_copy():
        return remote(C1.at[pl.ds(0, 16)], C1.at[pl.ds(16, 16)], cp_sem.at[0], cp_sem.at[1],
                      partner)

    def c1_own():
        return pltpu.make_async_copy(cache_ref.at[0, piece(chip), :], C1.at[chip], c_sem.at[4])

    def cache_start():
        def c1_start(o):
            @pl.when(lax.rem(chip + o, 16) < PIECES)
            def _():
                c1_copy(o).start()

        loop(1, 16, c1_start)

        @pl.when(serves)
        def _():
            c1_own().start()

    def w_copies(i, g):
        slot = lax.rem(3 * i + g, SLOTS)
        j = 5 * g + i
        out = []
        for h in range(2):
            half = c if h == 0 else 1 - c
            row = pl.multiple_of(half * HALF + j * LANES, LANES)
            for m, src in enumerate((wg_ref, wu_ref)):
                out.append(pltpu.make_async_copy(
                    src.at[0, pl.ds(row, LANES), :],
                    Wgu.at[slot, pl.ds(h * LANES, LANES), pl.ds(m * 512, 512)],
                    w_sem.at[slot]))
        return out

    def wd_copies(j):
        out = []
        for h in range(2):
            half = c if h == 0 else 1 - c
            col = pl.multiple_of(half * HALF + j * LANES, LANES)
            out.append(pltpu.make_async_copy(
                wd_ref.at[0, :, pl.ds(col, LANES)],
                Wd.at[j, :, pl.ds(h * LANES, LANES)],
                wd_sem.at[j]))
        return out

    for i in range(2):
        for g in range(3):
            for cp in w_copies(i, g):
                cp.start()

    def two(v):
        mine = lax.broadcasted_iota(jnp.int32, (16, v.shape[1]), 0) // 8 == c
        return jnp.where(mine, jnp.concatenate([v, v], axis=0), 0.0).astype(bf16)

    loads[0].wait()
    for h in range(2):
        for t in range(NOUT):
            lane = slice(h * HALF + t * LANES, h * HALF + (t + 1) * LANES)
            xin[h, :, t * LANES:(t + 1) * LANES] = two(hid_ref[:, lane].astype(f32))

    pl.semaphore_wait(barrier, 37)

    swap = remote(xin.at[1 - c], xr, x_sem.at[0], x_sem.at[1], partner)
    swap.start()
    cache_start()
    for cp in loads[1:]:
        cp.wait()
    score = 1.0 / (1.0 + jnp.exp(-scores_ref[...]))
    weight = 2.5 * score / jnp.sum(score, axis=1, keepdims=True)
    ids = ids_ref[...]
    lane8 = lax.broadcasted_iota(jnp.int32, (8, 128), 1)
    dense = jnp.zeros((8, 128), f32)
    for k in range(8):
        dense += jnp.where(ids[:, k:k + 1] == lane8 % 32, weight[:, k:k + 1], 0.0)
    hi = dense.astype(bf16).astype(f32)
    mid = (dense - hi).astype(bf16).astype(f32)
    low = dense - hi - mid
    part = lane8 // 32
    extra = jnp.where(part == 0, hi, jnp.where(part == 1, mid, jnp.where(part == 2, low, 0.0)))

    ext[...] = two(extra)
    swap2 = remote(ext, extr, x_sem.at[2], x_sem.at[3], partner)
    swap2.start()

    swap.wait()
    for j in range(NOUT):
        lane = slice(j * LANES, (j + 1) * LANES)
        X[j, me["z"], me["x"], me["y"], :, 0:LANES] = xin[c, :, lane] + xr[:, lane]

    PEERS = (1, -1, 2)

    def ag_copy(g, stage, part, q):
        a = ORDER[g][stage]
        done = ORDER[g][:stage]
        spec = {b: (slice(None) if b in done else me[b]) for b in AX}
        rows = pl.ds(5 * g, 1) if part == 0 else pl.ds(5 * g + 1, 4)
        ref = X.at[rows, spec["z"], spec["x"], spec["y"], :, pl.ds(0, LANES)]
        return remote(ref, ref, ag_s.at[stage], ag_r.at[stage, part],
                      peer(a, PEERS[q]))

    def ag3_copy(g, kind, i):
        a = ORDER[g][2]
        done = [b for b in AX if b != a]
        spec = {b: slice(None) for b in AX}
        spec[a] = mod4(me[a] + (0, 0, -1, 1)[kind])
        if kind >= 2:
            spec[done[0]] = pl.ds((kind - 2) * 2, 2)
        j = 5 * g + i
        ref = X.at[j, spec["z"], spec["x"], spec["y"], :, pl.ds(0, LANES)]
        return remote(ref, ref, ag3_s, ag3_r.at[j, kind // 2],
                      peer(a, 1 if kind % 2 == 0 else -1))

    def ag_partner(j):
        return remote(
            X.at[j, :, :, :, :, pl.ds(0, LANES)], X.at[j, :, :, :, :, pl.ds(LANES, LANES)],
            agp_s, agp_r.at[j], partner)

    def ag_all(stage, part, act):
        for g in range(3):
            for q in range(3):
                act(ag_copy(g, stage, part, q))

    def start(cp):
        cp.start()

    def ag_take(stage, part):
        ref = X.at[pl.ds(0, 9), 0, pl.ds(0, 4 ** part), pl.ds(0, 4 ** stage), :, pl.ds(0, LANES)]
        take(ag_r.at[stage, part], ref)

    def ag3_take(i, g, k):
        a = ORDER[g][2]
        spec = {b: slice(None) for b in AX}
        spec[a] = pl.ds(0, 2 - k)
        take(ag3_r.at[5 * g + i, k],
             X.at[5 * g + i, spec["z"], spec["x"], spec["y"], :, pl.ds(0, LANES)])

    ag_all(0, 0, start)
    swap2.wait()
    X[14, me["z"], me["x"], me["y"], :, 0:128] = ext[...] + extr[...]
    X[14, me["z"], me["x"], me["y"], :, 128:256] = jnp.zeros((16, 128), bf16)
    ag_all(0, 1, start)

    def wd_start(j):
        for cp in wd_copies(j):
            cp.start()

    acc[...] = jnp.zeros_like(acc)

    def find(k):
        d = 2 * k + c
        src = jnp.int32(0)
        for q in range(32):
            src = jnp.where(plan_ref[q] == d, jnp.int32(q), src)
        order_ref[k] = lax.rem(lax.rem(src, 2) + c, 2) * 16 + src // 2

    ag_take(0, 0)
    ag_all(1, 0, start)
    ag_take(0, 1)
    ag_all(1, 1, start)

    loop(0, 16, find)

    def ag3_start(i):
        for g in range(3):
            for kind in range(2):
                ag3_copy(g, kind, i).start()

    ag_take(1, 0)
    ag3_start(0)
    ag_take(1, 1)
    ag3_start(1)

    def valid(i, g):
        return (i >= 0) & (i < (4 if g == 2 else 5))

    def gate_up(i, g):
        j = 5 * g + i
        slot = lax.rem(3 * i + g, SLOTS)
        take(w_sem.at[slot], Wgu.at[slot])

        for zi in range(4):
            xb = X[j, zi].reshape(256, 512)
            acc[zi] += jnp.dot(xb, Wgu[slot], preferred_element_type=f32)

        @pl.when(valid(i + 2, g))
        def _():
            for cp in w_copies(i + 2, g):
                cp.start()

    def ag_step(i):
        for g in range(3):
            @pl.when(i < 5)
            def _():
                ag3_take(i, g, 0)
                for kind in range(2):
                    ag3_copy(g, kind + 2, i).start()

            @pl.when(i + 2 < 5)
            def _():
                for kind in range(2):
                    ag3_copy(g, kind, i + 2).start()

            @pl.when(valid(i - 2, g))
            def _():
                ag_partner(5 * g + i - 2).wait_recv()
                gate_up(i - 2, g)

            @pl.when((i >= 1) & (i < 6))
            def _():
                ag3_take(i - 1, g, 1)

            @pl.when(valid(i - 1, g))
            def _():
                ag_partner(5 * g + i - 1).start()

        @pl.when(i == 1)
        def _():
            loop(0, NOUT, wd_start)

        @pl.when(i == 2)
        def _():
            @pl.when(serves)
            def _():
                take(c_sem.at[1], C1.at[pl.ds(0, 15)])
                c1_own().wait()
                cp_copy().start()

        @pl.when(i == 5)
        def _():
            @pl.when(serves)
            def _():
                cp_copy().wait()

                def reorder(k):
                    C2[k] = C1[order_ref[k]]

                loop(0, 16, reorder)
                loop(1, 16, lambda o: c2_copy(o).start())
                co_ref[piece(chip), :] = C2[chip]

    loop(0, 7, ag_step)

    low_lanes = pl.ds(0, LANES)
    take(ag_s.at[0], X.at[:, 0, 0, pl.ds(0, 3), :, low_lanes])
    take(ag_s.at[1], X.at[:, 0, pl.ds(0, 3), :, :, low_lanes])
    take(ag3_s, X.at[:, pl.ds(0, 3), :, :, :, low_lanes])
    take(agp_s, X.at[pl.ds(0, NOUT), :, :, :, :, low_lanes])

    lane_id = lax.broadcasted_iota(jnp.int32, (128, 128), 0)
    pick = jnp.where((lax.rem(lane_id, 32) == dec) & (lane_id < 96), 1.0, 0.0).astype(bf16)

    def hidden_rows(zi):
        gate = acc[zi, :, 0:512]
        up = acc[zi, :, 512:1024]
        H[zi] = (gate / (1.0 + jnp.exp(-gate)) * up).astype(bf16)
        wb[zi] = jnp.dot(X[14, zi, :, :, :, 0:128].reshape(256, 128), pick,
                         preferred_element_type=f32)

    loop(0, 4, hidden_rows)

    def rp_copy(j):
        return remote(X.at[j, :, :, :, :, pl.ds(LANES, LANES)], R.at[j], rp_s, rp_r.at[j],
                      partner)

    def down(i, g):
        j = 5 * g + i
        take(wd_sem.at[j], Wd.at[j])

        w = wb[...].reshape(1024, 128)
        w = jnp.concatenate([w, w], axis=1)
        for h in (1, 0):
            lane = slice(h * LANES, (h + 1) * LANES)
            out = jnp.dot(H[...].reshape(1024, 512), Wd[j, :, lane], preferred_element_type=f32)
            X[j, :, :, :, :, lane] = (out * w).astype(bf16).reshape(4, 4, 4, 16, LANES)
            if h:
                rp_copy(j).start()

    def chip_sum(j):
        rp_copy(j).wait_recv()

        def rows(zi):
            X[j, zi, :, :, :, 0:LANES] += R[j, zi]

        loop(0, 4, rows)

    def plane_of(g, j, at, half=None):
        a = ORDER[g][2]
        rest = [b for b in AX if b != a]
        spec = {b: slice(None) for b in AX}
        spec[a] = at
        if half is not None:
            spec[rest[0]] = pl.ds(2 * half, 2)
        return X.at[j, spec["z"], spec["x"], spec["y"], :, pl.ds(0, LANES)]

    def rs_copy(g, kind, j):
        a = ORDER[g][2]
        p = me[a]
        if kind < 2:
            src, dst = plane_of(g, j, mod4(p + 2), kind), RA1.at[kind, j]
        else:
            src, dst = plane_of(g, j, mod4(p + (1 if kind == 2 else -1))), RA2.at[kind - 2, j]
        return remote(src, dst, rs_s.at[kind // 2], rs_r.at[j, kind // 2],
                      peer(a, 1 if kind % 2 == 0 else -1))

    def line_of(g, stage, j, at):
        if stage == 0:
            rest = [b for b in AX if b != ORDER[g][2]]
            return T.at[j, at] if rest[0] == ORDER[g][1] else T.at[j, :, at]
        return U.at[j, at]

    def rb_copy(g, stage, q, j):
        a = ORDER[g][1 - stage]
        src = line_of(g, stage, j, mod4(me[a] + PEERS[q]))
        return remote(src, (RB, RC)[stage].at[q, j], rb_s.at[stage], rb_r.at[j, stage],
                      peer(a, PEERS[q]))

    def tail_piece(g, j, o):
        a1, a2, a3 = ORDER[g]
        at = {a1: mod4(me[a1] + o // 4), a2: mod4(me[a2] + o % 4)}
        rest = [b for b in AX if b != a3]
        return T.at[j, at[rest[0]], at[rest[1]]]

    def tail_start(g, j):
        def one(q):
            o = 16 - q
            remote(tail_piece(g, j, o), RT.at[g, o - 1], rt_s, rt_r.at[g],
                   mate(ORDER[g][0], ORDER[g][1], o)).start()

        loop(1, 16, one)

    def tail_last(g, j):
        take(rt_r.at[g], RT.at[g])
        total = tail_piece(g, j, 0)[...].astype(f32)
        for o in range(15):
            total = total + RT[g, o].astype(f32)
        finish(j, total)

    def tail(i, g):
        return i == (3 if g == 2 else 4)

    def early(i, g):
        return (i >= 0) & (i < (3 if g == 2 else 4))

    def rs_first(g, j):
        for kind in range(2):
            rs_copy(g, kind, j).start()

    def rs_second(g, j):
        p = me[ORDER[g][2]]
        take(rs_r.at[j, 0], RA1.at[:, j])
        for kind in range(2):
            ref = plane_of(g, j, mod4(p + (1 if kind == 0 else -1)), kind)
            ref[...] += RA1[kind, j]
            rs_copy(g, kind + 2, j).start()

    def rs_last(g, j):
        take(rs_r.at[j, 1], RA2.at[:, j])
        total = (plane_of(g, j, me[ORDER[g][2]])[...].astype(f32) + RA2[0, j].astype(f32)
                 + RA2[1, j].astype(f32))
        T[j] = total.astype(bf16)

    def rb_start(g, stage, j):
        for q in range(3):
            rb_copy(g, stage, q, j).start()

    def rb_last(g, stage, j):
        buf = (RB, RC)[stage]
        take(rb_r.at[j, stage], buf.at[:, j])
        total = line_of(g, stage, j, me[ORDER[g][1 - stage]])[...].astype(f32)
        for q in range(3):
            total = total + buf[q, j].astype(f32)
        if stage == 0:
            U[j] = total.astype(bf16)
        else:
            finish(j, total)

    def finish(j, total):
        first = c == 0
        mine = jnp.where(first, total[0:8], total[8:16])
        FS[j] = jnp.where(first, total[8:16], total[0:8])
        moe_ref[:, pl.ds(pl.multiple_of(c * HALF + j * LANES, LANES), LANES)] = mine.astype(bf16)

    def co_out():
        return pltpu.make_async_copy(co_ref, co_hbm.at[0], io_sem.at[5])

    def hand_over():
        length = jnp.int32(0)
        for q in range(32):
            length = jnp.where(plan_ref[q] == dec, plen_ref[q], length)

        @pl.when(serves)
        def _():
            take(c_sem.at[3], C2.at[pl.ds(0, PIECES - 1)])

        @pl.when(jnp.logical_not(serves))
        def _():
            take(c_sem.at[3], C2.at[pl.ds(0, PIECES)])


        def mask_rows(k):
            pos = y * 256 + lax.broadcasted_iota(jnp.int32, (48, 256), 1)
            kept = co_ref[piece(k), :].astype(f32)
            co_ref[piece(k), :] = jnp.where(pos < length, kept, 0.0).astype(bf16)

        loop(0, PIECES, mask_rows)
        co_out().start()

    def rs_step(i):
        @pl.when(i == 4)
        def _():
            hand_over()

        for g in range(3):
            @pl.when(valid(i, g))
            def _():
                down(i, g)

            ib, gb = (i, g - 1) if g else (i - 1, 2)

            @pl.when(early(ib - 4, gb))
            def _():
                rb_last(gb, 1, 5 * gb + ib - 4)

            @pl.when(tail(ib - 3, gb))
            def _():
                tail_last(gb, 5 * gb + ib - 3)

            @pl.when(early(ib - 3, gb))
            def _():
                rb_last(gb, 0, 5 * gb + ib - 3)
                rb_start(gb, 1, 5 * gb + ib - 3)

            @pl.when(valid(ib - 2, gb))
            def _():
                rs_last(gb, 5 * gb + ib - 2)

            @pl.when(early(ib - 2, gb))
            def _():
                rb_start(gb, 0, 5 * gb + ib - 2)

            @pl.when(tail(ib - 2, gb))
            def _():
                tail_start(gb, 5 * gb + ib - 2)

            @pl.when(valid(ib - 1, gb))
            def _():
                rs_second(gb, 5 * gb + ib - 1)

            @pl.when(valid(ib, gb))
            def _():
                chip_sum(5 * gb + ib)
                rs_first(gb, 5 * gb + ib)

    loop(0, 8, rs_step)

    fo = remote(FS, FR, fo_sem.at[0], fo_sem.at[1], partner)
    fo.start()

    @pl.when(serves)
    def _():
        take(c_sem.at[0], C2.at[pl.ds(0, PIECES - 1)])
        take(c_sem.at[2], C2.at[pl.ds(0, 15)])

    @pl.when(jnp.logical_not(serves))
    def _():
        take(c_sem.at[0], C2.at[pl.ds(0, PIECES)])

    take(rp_s, R)
    take(rs_s.at[0], RA1)
    take(rs_s.at[1], RA2)
    take(rb_s.at[0], RB.at[:, pl.ds(0, NOUT - 3)])
    take(rb_s.at[1], RC.at[:, pl.ds(0, NOUT - 3)])
    take(rt_s, RT)
    fo.wait()
    for j in range(NOUT):
        moe_ref[:, pl.ds(pl.multiple_of((1 - c) * HALF + j * LANES, LANES), LANES)] = (
            FR[j].astype(bf16))
    moe_out = pltpu.make_async_copy(moe_ref, moe_hbm, io_sem.at[6])
    moe_out.start()
    co_out().wait()
    moe_out.wait()


def body(
    hidden_states, gate_scores, expert_ids, w_gate, w_up, w_down, prefill_cache, plan, prompt_len
):
    hbm = pl.BlockSpec(memory_space=pl.ANY)
    dma = pltpu.SemaphoreType.DMA
    moe, handed = pl.pallas_call(
        kernel,
        out_shape=(
            jax.ShapeDtypeStruct((8, 7168), bf16),
            jax.ShapeDtypeStruct((1, 576, 256), bf16),
        ),
        in_specs=[hbm] * 9,
        out_specs=(hbm, hbm),
        scratch_shapes=[
            pltpu.VMEM((NCH, 4, 4, 4, 16, 512), bf16),
            pltpu.VMEM((2, 16, HALF), bf16),
            pltpu.VMEM((16, HALF), bf16),
            pltpu.VMEM((16, 128), bf16),
            pltpu.VMEM((16, 128), bf16),
            pltpu.VMEM((SLOTS, 512, 1024), bf16),
            pltpu.VMEM((NOUT, 512, 512), bf16),
            pltpu.VMEM((4, 256, 1024), f32),
            pltpu.VMEM((4, 256, 512), bf16),
            pltpu.VMEM((4, 256, 128), f32),
            pltpu.VMEM((NOUT, 4, 4, 4, 16, LANES), bf16),
            pltpu.VMEM((2, NOUT, 2, 4, 16, LANES), bf16),
            pltpu.VMEM((2, NOUT, 4, 4, 16, LANES), bf16),
            pltpu.VMEM((NOUT, 4, 4, 16, LANES), bf16),
            pltpu.VMEM((3, NOUT, 4, 16, LANES), bf16),
            pltpu.VMEM((NOUT, 4, 16, LANES), bf16),
            pltpu.VMEM((3, NOUT, 16, LANES), bf16),
            pltpu.VMEM((3, 15, 16, LANES), bf16),
            pltpu.VMEM((NOUT, 8, LANES), f32),
            pltpu.VMEM((NOUT, 8, LANES), f32),
            pltpu.VMEM((32, 48, 256), bf16),
            pltpu.VMEM((16, 48, 256), bf16),
            pltpu.SMEM((16,), jnp.int32),
            pltpu.SMEM((32,), jnp.int32),
            pltpu.SMEM((32,), jnp.int32),
            pltpu.VMEM((8, 8), f32),
            pltpu.VMEM((8, 8), jnp.int32),
            pltpu.VMEM((8, 7168), bf16),
            pltpu.VMEM((8, 7168), bf16),
            pltpu.VMEM((576, 256), bf16),
            dma((7,)),
            dma((4,)),
            dma((2,)), dma((2, 2)),
            dma, dma((NCH, 2)),
            dma, dma((NOUT,)),
            dma((SLOTS,)), dma((NOUT,)),
            dma, dma((NOUT,)),
            dma((2,)), dma((NOUT, 2)),
            dma((2,)), dma((NOUT, 2)),
            dma, dma((3,)),
            dma((2,)),
            dma((5,)),
            dma((2,)),
        ],
        compiler_params=pltpu.CompilerParams(
            collective_id=0, has_side_effects=True, vmem_limit_bytes=60 * 1024 * 1024),
        cost_estimate=pl.CostEstimate(
            flops=22_500_000_000, bytes_accessed=23_000_000, transcendentals=524288),
    )(plan, prompt_len, gate_scores, expert_ids, hidden_states,
      jnp.swapaxes(prefill_cache, 1, 2), w_gate, w_up, w_down)

    def hand_on(moe_in, handed_in, moe_out, handed_out):
        moe_out[...] = moe_in[...]
        handed_out[...] = handed_in[...]

    vm = pl.BlockSpec(memory_space=pltpu.VMEM)
    moe, handed = pl.pallas_call(
        hand_on,
        out_shape=(
            jax.ShapeDtypeStruct((8, 7168), bf16),
            jax.ShapeDtypeStruct((1, 576, 256), bf16),
        ),
        in_specs=[vm, vm],
        out_specs=(vm, vm),
        cost_estimate=pl.CostEstimate(flops=0, bytes_accessed=820_000, transcendentals=0),
    )(moe, handed)
    return moe, jnp.swapaxes(handed, 1, 2)


def solution(mesh):
    in_specs = (
        P(("dec", "seq"), None),
        P(("dec", "seq"), None),
        P(("dec", "seq"), None),
        P("dec", None, "seq"),
        P("dec", None, "seq"),
        P("dec", "seq", None),
        P("dec", "seq", None),
        P(),
        P(),
    )
    out_specs = (P(("dec", "seq"), None), P("dec", "seq", None))
    return jax.shard_map(body, mesh=mesh, in_specs=in_specs, out_specs=out_specs, check_vma=False)
```

```python
import jax
import jax.numpy as jnp
from jax import lax
from jax.experimental import pallas as pl
from jax.experimental.pallas import tpu as pltpu
from jax.sharding import PartitionSpec as P

MESH = pl.DeviceIdType.MESH
AX = ("z", "x", "y")
ORDER = (("y", "x", "z"), ("z", "y", "x"), ("x", "z", "y"))
NCH = 15
NOUT = 14
LANES = 256
HALF = NOUT * LANES
SLOTS = 6
PIECES = 12
bf16 = jnp.bfloat16
f32 = jnp.float32


def mod4(v):
    return lax.rem(v + 8, 4)


def loop(lo, hi, fn):
    def step(k, carry):
        fn(k)
        return carry

    lax.fori_loop(lo, hi, step, 0)


def kernel(
    plan_hbm, plen_hbm, scores_hbm, ids_hbm, hid_hbm, cache_ref, wg_ref, wu_ref, wd_ref,
    moe_hbm, co_hbm,
    X, xin, xr, ext, extr, Wgu, Wd, acc, H, wb, R, RA1, RA2, T, RB, U, RC, RT, FS, FR, C1, C2, order_ref,
    plan_ref, plen_ref, scores_ref, ids_ref, hid_ref, moe_ref, co_ref, io_sem,
    x_sem, ag_s, ag_r, ag3_s, ag3_r, agp_s, agp_r, w_sem, wd_sem,
    rp_s, rp_r, rs_s, rs_r, rb_s, rb_r, rt_s, rt_r, fo_sem, c_sem, cp_sem,
):
    dec = lax.axis_index("dec")
    y = lax.axis_index("seq")
    c = lax.rem(dec, 2)
    chip = dec // 2
    me = {"z": dec // 8, "x": lax.rem(dec // 2, 4), "y": y}

    def dev(pos, core):
        return ((pos["z"] * 4 + pos["x"]) * 2 + core, pos["y"])

    def peer(a, d):
        pos = dict(me)
        pos[a] = mod4(me[a] + d)
        return dev(pos, c)

    def mate(a, b, o):
        pos = dict(me)
        pos[a] = mod4(me[a] + o // 4)
        pos[b] = mod4(me[b] + o % 4)
        return dev(pos, c)

    partner = dev(me, 1 - c)

    def plane_id(o):
        return (lax.rem(chip + o, 16) * 2 + c, y)

    def remote(src, dst, s, r, to):
        return pltpu.make_async_remote_copy(src, dst, s, r, device_id=to, device_id_type=MESH)

    loads = [pltpu.make_async_copy(src, dst, io_sem.at[q]) for q, (src, dst) in enumerate((
        (hid_hbm, hid_ref), (scores_hbm, scores_ref), (ids_hbm, ids_ref),
        (plan_hbm, plan_ref), (plen_hbm, plen_ref)))]
    for cp in loads:
        cp.start()

    def take(sem, ref):
        pltpu.make_async_copy(ref, ref, sem).wait()

    barrier = pltpu.get_barrier_semaphore()
    for o in range(1, 16):
        pl.semaphore_signal(barrier, inc=1, device_id=plane_id(o), device_id_type=MESH)
    for o in range(4, 16):
        pl.semaphore_signal(barrier, inc=1, device_id=mate("y", "x", o), device_id_type=MESH)
    for o in range(5, 16):
        if o % 4:
            pl.semaphore_signal(barrier, inc=1, device_id=mate("z", "y", o), device_id_type=MESH)
    pl.semaphore_signal(barrier, inc=1, device_id=partner, device_id_type=MESH)

    def piece(k):
        return pl.ds(pl.multiple_of(k * 48, 16), 48)

    serves = chip < PIECES

    def c1_copy(o):
        to = lax.rem(chip + o, 16)
        return remote(cache_ref.at[0, piece(to), :], C1.at[chip], c_sem.at[0], c_sem.at[1],
                      plane_id(o))

    def c2_copy(o):
        to = lax.rem(chip + o, 16)
        return remote(C2.at[to], co_ref.at[piece(chip), :], c_sem.at[2], c_sem.at[3],
                      plane_id(o))

    def cp_copy():
        return remote(C1.at[pl.ds(0, 16)], C1.at[pl.ds(16, 16)], cp_sem.at[0], cp_sem.at[1],
                      partner)

    def c1_own():
        return pltpu.make_async_copy(cache_ref.at[0, piece(chip), :], C1.at[chip], c_sem.at[4])

    def cache_start():
        def c1_start(o):
            @pl.when(lax.rem(chip + o, 16) < PIECES)
            def _():
                c1_copy(o).start()

        loop(1, 16, c1_start)

        @pl.when(serves)
        def _():
            c1_own().start()

    def w_copies(i, g):
        slot = lax.rem(3 * i + g, SLOTS)
        j = 5 * g + i
        out = []
        for h in range(2):
            half = c if h == 0 else 1 - c
            row = pl.multiple_of(half * HALF + j * LANES, LANES)
            for m, src in enumerate((wg_ref, wu_ref)):
                out.append(pltpu.make_async_copy(
                    src.at[0, pl.ds(row, LANES), :],
                    Wgu.at[slot, pl.ds(h * LANES, LANES), pl.ds(m * 512, 512)],
                    w_sem.at[slot]))
        return out

    def wd_copies(j):
        out = []
        for h in range(2):
            half = c if h == 0 else 1 - c
            col = pl.multiple_of(half * HALF + j * LANES, LANES)
            out.append(pltpu.make_async_copy(
                wd_ref.at[0, :, pl.ds(col, LANES)],
                Wd.at[j, :, pl.ds(h * LANES, LANES)],
                wd_sem.at[j]))
        return out

    for i in range(2):
        for g in range(3):
            for cp in w_copies(i, g):
                cp.start()

    def two(v):
        mine = lax.broadcasted_iota(jnp.int32, (16, v.shape[1]), 0) // 8 == c
        return jnp.where(mine, jnp.concatenate([v, v], axis=0), 0.0).astype(bf16)

    loads[0].wait()
    for h in range(2):
        for t in range(NOUT):
            lane = slice(h * HALF + t * LANES, h * HALF + (t + 1) * LANES)
            xin[h, :, t * LANES:(t + 1) * LANES] = two(hid_ref[:, lane].astype(f32))

    pl.semaphore_wait(barrier, 37)

    swap = remote(xin.at[1 - c], xr, x_sem.at[0], x_sem.at[1], partner)
    swap.start()
    cache_start()
    for cp in loads[1:]:
        cp.wait()
    score = 1.0 / (1.0 + jnp.exp(-scores_ref[...]))
    weight = 2.5 * score / jnp.sum(score, axis=1, keepdims=True)
    ids = ids_ref[...]
    lane8 = lax.broadcasted_iota(jnp.int32, (8, 128), 1)
    dense = jnp.zeros((8, 128), f32)
    for k in range(8):
        dense += jnp.where(ids[:, k:k + 1] == lane8 % 32, weight[:, k:k + 1], 0.0)
    hi = dense.astype(bf16).astype(f32)
    mid = (dense - hi).astype(bf16).astype(f32)
    low = dense - hi - mid
    part = lane8 // 32
    extra = jnp.where(part == 0, hi, jnp.where(part == 1, mid, jnp.where(part == 2, low, 0.0)))

    ext[...] = two(extra)
    swap2 = remote(ext, extr, x_sem.at[2], x_sem.at[3], partner)
    swap2.start()

    swap.wait()
    for j in range(NOUT):
        lane = slice(j * LANES, (j + 1) * LANES)
        X[j, me["z"], me["x"], me["y"], :, 0:LANES] = xin[c, :, lane] + xr[:, lane]

    PEERS = (1, -1, 2)

    def ag_copy(g, stage, part, q):
        a = ORDER[g][stage]
        done = ORDER[g][:stage]
        spec = {b: (slice(None) if b in done else me[b]) for b in AX}
        rows = pl.ds(5 * g, 1) if part == 0 else pl.ds(5 * g + 1, 4)
        ref = X.at[rows, spec["z"], spec["x"], spec["y"], :, pl.ds(0, LANES)]
        return remote(ref, ref, ag_s.at[stage], ag_r.at[stage, part],
                      peer(a, PEERS[q]))

    def ag3_copy(g, kind, i):
        a = ORDER[g][2]
        done = [b for b in AX if b != a]
        spec = {b: slice(None) for b in AX}
        spec[a] = mod4(me[a] + (0, 0, -1, 1)[kind])
        if kind >= 2:
            spec[done[0]] = pl.ds((kind - 2) * 2, 2)
        j = 5 * g + i
        ref = X.at[j, spec["z"], spec["x"], spec["y"], :, pl.ds(0, LANES)]
        return remote(ref, ref, ag3_s, ag3_r.at[j, kind // 2],
                      peer(a, 1 if kind % 2 == 0 else -1))

    def ag_partner(g, i, d):
        j = 5 * g + i
        spec = {b: slice(None) for b in AX}
        spec[ORDER[g][2]] = mod4(me[ORDER[g][2]] + d)
        at = (j, spec["z"], spec["x"], spec["y"], slice(None))
        return remote(X.at[(*at, pl.ds(0, LANES))], X.at[(*at, pl.ds(LANES, LANES))],
                      agp_s, agp_r.at[j], partner)

    def ag_all(stage, part, act):
        for g in range(3):
            for q in range(3):
                act(ag_copy(g, stage, part, q))

    def start(cp):
        cp.start()

    def ag_take(stage, part):
        ref = X.at[pl.ds(0, 9), 0, pl.ds(0, 4 ** part), pl.ds(0, 4 ** stage), :, pl.ds(0, LANES)]
        take(ag_r.at[stage, part], ref)

    def ag3_take(i, g, k):
        a = ORDER[g][2]
        spec = {b: slice(None) for b in AX}
        spec[a] = pl.ds(0, 2 - k)
        take(ag3_r.at[5 * g + i, k],
             X.at[5 * g + i, spec["z"], spec["x"], spec["y"], :, pl.ds(0, LANES)])

    ag_all(0, 0, start)
    swap2.wait()
    X[14, me["z"], me["x"], me["y"], :, 0:128] = ext[...] + extr[...]
    X[14, me["z"], me["x"], me["y"], :, 128:256] = jnp.zeros((16, 128), bf16)
    ag_all(0, 1, start)

    def wd_start(j):
        for cp in wd_copies(j):
            cp.start()

    acc[...] = jnp.zeros_like(acc)

    def find(k):
        d = 2 * k + c
        src = jnp.int32(0)
        for q in range(32):
            src = jnp.where(plan_ref[q] == d, jnp.int32(q), src)
        order_ref[k] = lax.rem(lax.rem(src, 2) + c, 2) * 16 + src // 2

    ag_take(0, 0)
    ag_all(1, 0, start)
    ag_take(0, 1)
    ag_all(1, 1, start)

    loop(0, 16, find)

    def ag3_start(i):
        for g in range(3):
            for kind in range(2):
                ag3_copy(g, kind, i).start()

    ag_take(1, 0)
    ag3_start(0)
    ag_take(1, 1)
    ag3_start(1)

    def valid(i, g):
        return (i >= 0) & (i < (4 if g == 2 else 5))

    def gate_up(i, g):
        j = 5 * g + i
        slot = lax.rem(3 * i + g, SLOTS)
        take(w_sem.at[slot], Wgu.at[slot])

        for zi in range(4):
            xb = X[j, zi].reshape(256, 512)
            acc[zi] += jnp.dot(xb, Wgu[slot], preferred_element_type=f32)

        @pl.when(valid(i + 2, g))
        def _():
            for cp in w_copies(i + 2, g):
                cp.start()

    def ag_step(i):
        for g in range(3):
            @pl.when(i < 5)
            def _():
                ag3_take(i, g, 0)
                for kind in range(2):
                    ag3_copy(g, kind + 2, i).start()

            @pl.when(valid(i, g))
            def _():
                for d in (0, -1, 1):
                    ag_partner(g, i, d).start()

            @pl.when(i + 2 < 5)
            def _():
                for kind in range(2):
                    ag3_copy(g, kind, i + 2).start()

            @pl.when(valid(i - 2, g))
            def _():
                j = 5 * g + i - 2
                take(agp_r.at[j], X.at[j, :, :, :, :, pl.ds(LANES, LANES)])
                gate_up(i - 2, g)

            @pl.when((i >= 1) & (i < 6))
            def _():
                ag3_take(i - 1, g, 1)

            @pl.when(valid(i - 1, g))
            def _():
                ag_partner(g, i - 1, 2).start()

        @pl.when(i == 1)
        def _():
            loop(0, NOUT, wd_start)

        @pl.when(i == 2)
        def _():
            @pl.when(serves)
            def _():
                take(c_sem.at[1], C1.at[pl.ds(0, 15)])
                c1_own().wait()
                cp_copy().start()

        @pl.when(i == 5)
        def _():
            @pl.when(serves)
            def _():
                cp_copy().wait()

                def reorder(k):
                    C2[k] = C1[order_ref[k]]

                loop(0, 16, reorder)
                loop(1, 16, lambda o: c2_copy(o).start())
                co_ref[piece(chip), :] = C2[chip]

    loop(0, 7, ag_step)

    low_lanes = pl.ds(0, LANES)
    take(ag_s.at[0], X.at[:, 0, 0, pl.ds(0, 3), :, low_lanes])
    take(ag_s.at[1], X.at[:, 0, pl.ds(0, 3), :, :, low_lanes])
    take(ag3_s, X.at[:, pl.ds(0, 3), :, :, :, low_lanes])
    take(agp_s, X.at[pl.ds(0, NOUT), :, :, :, :, low_lanes])

    lane_id = lax.broadcasted_iota(jnp.int32, (128, 128), 0)
    pick = jnp.where((lax.rem(lane_id, 32) == dec) & (lane_id < 96), 1.0, 0.0).astype(bf16)

    def hidden_rows(zi):
        gate = acc[zi, :, 0:512]
        up = acc[zi, :, 512:1024]
        H[zi] = (gate / (1.0 + jnp.exp(-gate)) * up).astype(bf16)
        wb[zi] = jnp.dot(X[14, zi, :, :, :, 0:128].reshape(256, 128), pick,
                         preferred_element_type=f32)

    loop(0, 4, hidden_rows)

    def rp_copy(j):
        return remote(X.at[j, :, :, :, :, pl.ds(LANES, LANES)], R.at[j], rp_s, rp_r.at[j],
                      partner)

    def down(i, g):
        j = 5 * g + i
        take(wd_sem.at[j], Wd.at[j])

        w = wb[...].reshape(1024, 128)
        w = jnp.concatenate([w, w], axis=1)
        for h in (1, 0):
            lane = slice(h * LANES, (h + 1) * LANES)
            out = jnp.dot(H[...].reshape(1024, 512), Wd[j, :, lane], preferred_element_type=f32)
            X[j, :, :, :, :, lane] = (out * w).astype(bf16).reshape(4, 4, 4, 16, LANES)
            if h:
                rp_copy(j).start()

    def chip_sum(j):
        rp_copy(j).wait_recv()

        def rows(zi):
            X[j, zi, :, :, :, 0:LANES] += R[j, zi]

        loop(0, 4, rows)

    def plane_of(g, j, at, half=None):
        a = ORDER[g][2]
        rest = [b for b in AX if b != a]
        spec = {b: slice(None) for b in AX}
        spec[a] = at
        if half is not None:
            spec[rest[0]] = pl.ds(2 * half, 2)
        return X.at[j, spec["z"], spec["x"], spec["y"], :, pl.ds(0, LANES)]

    def rs_copy(g, kind, j):
        a = ORDER[g][2]
        p = me[a]
        if kind < 2:
            src, dst = plane_of(g, j, mod4(p + 2), kind), RA1.at[kind, j]
        else:
            src, dst = plane_of(g, j, mod4(p + (1 if kind == 2 else -1))), RA2.at[kind - 2, j]
        return remote(src, dst, rs_s.at[kind // 2], rs_r.at[j, kind // 2],
                      peer(a, 1 if kind % 2 == 0 else -1))

    def line_of(g, stage, j, at):
        if stage == 0:
            rest = [b for b in AX if b != ORDER[g][2]]
            return T.at[j, at] if rest[0] == ORDER[g][1] else T.at[j, :, at]
        return U.at[j, at]

    def rb_copy(g, stage, q, j):
        a = ORDER[g][1 - stage]
        src = line_of(g, stage, j, mod4(me[a] + PEERS[q]))
        return remote(src, (RB, RC)[stage].at[q, j], rb_s.at[stage], rb_r.at[j, stage],
                      peer(a, PEERS[q]))

    def tail_piece(g, j, o):
        a1, a2, a3 = ORDER[g]
        at = {a1: mod4(me[a1] + o // 4), a2: mod4(me[a2] + o % 4)}
        rest = [b for b in AX if b != a3]
        return T.at[j, at[rest[0]], at[rest[1]]]

    def tail_start(g, j):
        def one(q):
            o = 16 - q
            remote(tail_piece(g, j, o), RT.at[g, o - 1], rt_s, rt_r.at[g],
                   mate(ORDER[g][0], ORDER[g][1], o)).start()

        loop(1, 16, one)

    def tail_last(g, j):
        take(rt_r.at[g], RT.at[g])
        total = tail_piece(g, j, 0)[...].astype(f32)
        for o in range(15):
            total = total + RT[g, o].astype(f32)
        finish(j, total)

    def tail(i, g):
        return i == (3 if g == 2 else 4)

    def early(i, g):
        return (i >= 0) & (i < (3 if g == 2 else 4))

    def rs_first(g, j):
        for kind in range(2):
            rs_copy(g, kind, j).start()

    def rs_second(g, j):
        p = me[ORDER[g][2]]
        take(rs_r.at[j, 0], RA1.at[:, j])
        for kind in range(2):
            ref = plane_of(g, j, mod4(p + (1 if kind == 0 else -1)), kind)
            ref[...] += RA1[kind, j]
            rs_copy(g, kind + 2, j).start()

    def rs_last(g, j):
        take(rs_r.at[j, 1], RA2.at[:, j])
        total = (plane_of(g, j, me[ORDER[g][2]])[...].astype(f32) + RA2[0, j].astype(f32)
                 + RA2[1, j].astype(f32))
        T[j] = total.astype(bf16)

    def rb_start(g, stage, j):
        for q in range(3):
            rb_copy(g, stage, q, j).start()

    def rb_last(g, stage, j):
        buf = (RB, RC)[stage]
        take(rb_r.at[j, stage], buf.at[:, j])
        total = line_of(g, stage, j, me[ORDER[g][1 - stage]])[...].astype(f32)
        for q in range(3):
            total = total + buf[q, j].astype(f32)
        if stage == 0:
            U[j] = total.astype(bf16)
        else:
            finish(j, total)

    def finish(j, total):
        first = c == 0
        mine = jnp.where(first, total[0:8], total[8:16])
        FS[j] = jnp.where(first, total[8:16], total[0:8])
        moe_ref[:, pl.ds(pl.multiple_of(c * HALF + j * LANES, LANES), LANES)] = mine.astype(bf16)

    def co_out():
        return pltpu.make_async_copy(co_ref, co_hbm.at[0], io_sem.at[5])

    def hand_over():
        length = jnp.int32(0)
        for q in range(32):
            length = jnp.where(plan_ref[q] == dec, plen_ref[q], length)

        @pl.when(serves)
        def _():
            take(c_sem.at[3], C2.at[pl.ds(0, PIECES - 1)])

        @pl.when(jnp.logical_not(serves))
        def _():
            take(c_sem.at[3], C2.at[pl.ds(0, PIECES)])


        def mask_rows(k):
            pos = y * 256 + lax.broadcasted_iota(jnp.int32, (48, 256), 1)
            kept = co_ref[piece(k), :].astype(f32)
            co_ref[piece(k), :] = jnp.where(pos < length, kept, 0.0).astype(bf16)

        loop(0, PIECES, mask_rows)
        co_out().start()

    def rs_step(i):
        @pl.when(i == 4)
        def _():
            hand_over()

        for g in range(3):
            @pl.when(valid(i, g))
            def _():
                down(i, g)

            ib, gb = (i, g - 1) if g else (i - 1, 2)

            @pl.when(early(ib - 4, gb))
            def _():
                rb_last(gb, 1, 5 * gb + ib - 4)

            @pl.when(tail(ib - 3, gb))
            def _():
                tail_last(gb, 5 * gb + ib - 3)

            @pl.when(early(ib - 3, gb))
            def _():
                rb_last(gb, 0, 5 * gb + ib - 3)
                rb_start(gb, 1, 5 * gb + ib - 3)

            @pl.when(valid(ib - 2, gb))
            def _():
                rs_last(gb, 5 * gb + ib - 2)

            @pl.when(early(ib - 2, gb))
            def _():
                rb_start(gb, 0, 5 * gb + ib - 2)

            @pl.when(tail(ib - 2, gb))
            def _():
                tail_start(gb, 5 * gb + ib - 2)

            @pl.when(valid(ib - 1, gb))
            def _():
                rs_second(gb, 5 * gb + ib - 1)

            @pl.when(valid(ib, gb))
            def _():
                chip_sum(5 * gb + ib)
                rs_first(gb, 5 * gb + ib)

    loop(0, 8, rs_step)

    fo = remote(FS, FR, fo_sem.at[0], fo_sem.at[1], partner)
    fo.start()

    @pl.when(serves)
    def _():
        take(c_sem.at[0], C2.at[pl.ds(0, PIECES - 1)])
        take(c_sem.at[2], C2.at[pl.ds(0, 15)])

    @pl.when(jnp.logical_not(serves))
    def _():
        take(c_sem.at[0], C2.at[pl.ds(0, PIECES)])

    take(rp_s, R)
    take(rs_s.at[0], RA1)
    take(rs_s.at[1], RA2)
    take(rb_s.at[0], RB.at[:, pl.ds(0, NOUT - 3)])
    take(rb_s.at[1], RC.at[:, pl.ds(0, NOUT - 3)])
    take(rt_s, RT)
    fo.wait()
    for j in range(NOUT):
        moe_ref[:, pl.ds(pl.multiple_of((1 - c) * HALF + j * LANES, LANES), LANES)] = (
            FR[j].astype(bf16))
    moe_out = pltpu.make_async_copy(moe_ref, moe_hbm, io_sem.at[6])
    moe_out.start()
    co_out().wait()
    moe_out.wait()


def body(
    hidden_states, gate_scores, expert_ids, w_gate, w_up, w_down, prefill_cache, plan, prompt_len
):
    hbm = pl.BlockSpec(memory_space=pl.ANY)
    dma = pltpu.SemaphoreType.DMA
    moe, handed = pl.pallas_call(
        kernel,
        out_shape=(
            jax.ShapeDtypeStruct((8, 7168), bf16),
            jax.ShapeDtypeStruct((1, 576, 256), bf16),
        ),
        in_specs=[hbm] * 9,
        out_specs=(hbm, hbm),
        scratch_shapes=[
            pltpu.VMEM((NCH, 4, 4, 4, 16, 512), bf16),
            pltpu.VMEM((2, 16, HALF), bf16),
            pltpu.VMEM((16, HALF), bf16),
            pltpu.VMEM((16, 128), bf16),
            pltpu.VMEM((16, 128), bf16),
            pltpu.VMEM((SLOTS, 512, 1024), bf16),
            pltpu.VMEM((NOUT, 512, 512), bf16),
            pltpu.VMEM((4, 256, 1024), f32),
            pltpu.VMEM((4, 256, 512), bf16),
            pltpu.VMEM((4, 256, 128), f32),
            pltpu.VMEM((NOUT, 4, 4, 4, 16, LANES), bf16),
            pltpu.VMEM((2, NOUT, 2, 4, 16, LANES), bf16),
            pltpu.VMEM((2, NOUT, 4, 4, 16, LANES), bf16),
            pltpu.VMEM((NOUT, 4, 4, 16, LANES), bf16),
            pltpu.VMEM((3, NOUT, 4, 16, LANES), bf16),
            pltpu.VMEM((NOUT, 4, 16, LANES), bf16),
            pltpu.VMEM((3, NOUT, 16, LANES), bf16),
            pltpu.VMEM((3, 15, 16, LANES), bf16),
            pltpu.VMEM((NOUT, 8, LANES), f32),
            pltpu.VMEM((NOUT, 8, LANES), f32),
            pltpu.VMEM((32, 48, 256), bf16),
            pltpu.VMEM((16, 48, 256), bf16),
            pltpu.SMEM((16,), jnp.int32),
            pltpu.SMEM((32,), jnp.int32),
            pltpu.SMEM((32,), jnp.int32),
            pltpu.VMEM((8, 8), f32),
            pltpu.VMEM((8, 8), jnp.int32),
            pltpu.VMEM((8, 7168), bf16),
            pltpu.VMEM((8, 7168), bf16),
            pltpu.VMEM((576, 256), bf16),
            dma((7,)),
            dma((4,)),
            dma((2,)), dma((2, 2)),
            dma, dma((NCH, 2)),
            dma, dma((NOUT,)),
            dma((SLOTS,)), dma((NOUT,)),
            dma, dma((NOUT,)),
            dma((2,)), dma((NOUT, 2)),
            dma((2,)), dma((NOUT, 2)),
            dma, dma((3,)),
            dma((2,)),
            dma((5,)),
            dma((2,)),
        ],
        compiler_params=pltpu.CompilerParams(
            collective_id=0, has_side_effects=True, vmem_limit_bytes=60 * 1024 * 1024),
        cost_estimate=pl.CostEstimate(
            flops=22_500_000_000, bytes_accessed=23_000_000, transcendentals=524288),
    )(plan, prompt_len, gate_scores, expert_ids, hidden_states,
      jnp.swapaxes(prefill_cache, 1, 2), w_gate, w_up, w_down)

    def hand_on(moe_in, handed_in, moe_out, handed_out):
        moe_out[...] = moe_in[...]
        handed_out[...] = handed_in[...]

    vm = pl.BlockSpec(memory_space=pltpu.VMEM)
    moe, handed = pl.pallas_call(
        hand_on,
        out_shape=(
            jax.ShapeDtypeStruct((8, 7168), bf16),
            jax.ShapeDtypeStruct((1, 576, 256), bf16),
        ),
        in_specs=[vm, vm],
        out_specs=(vm, vm),
        cost_estimate=pl.CostEstimate(flops=0, bytes_accessed=820_000, transcendentals=0),
    )(moe, handed)
    return moe, jnp.swapaxes(handed, 1, 2)


def solution(mesh):
    in_specs = (
        P(("dec", "seq"), None),
        P(("dec", "seq"), None),
        P(("dec", "seq"), None),
        P("dec", None, "seq"),
        P("dec", None, "seq"),
        P("dec", "seq", None),
        P("dec", "seq", None),
        P(),
        P(),
    )
    out_specs = (P(("dec", "seq"), None), P("dec", "seq", None))
    return jax.shard_map(body, mesh=mesh, in_specs=in_specs, out_specs=out_specs, check_vma=False)
```
